32 devices in a mesh: pipe: 4 (over z), dp: 8 (over y, x, core).
Axes of the slice: x: 2, y: 2, z: 4, core: 2. Of those that a mesh axis runs over, the one named last changes fastest.
Arguments:
- section_input: bfloat16 [4, 1024, 4096], P('pipe', 'dp'), may hold values from -6 to 6
- out_grad: bfloat16 [4, 1024, 4096], P('pipe', 'dp'), may hold values from -6 to 6
- short_filter: bfloat16 [4, 2, 7, 4096], P('pipe', None, None, 'dp'), may hold values from -2 to 2
- long_filter: bfloat16 [4, 2, 256, 128], P('pipe', None, 'dp'), may hold values from -0.5 to 0.5
Outputs:
- passed_grad: bfloat16 [4, 1024, 4096], P('pipe', 'dp')
- short_grad: float32 [4, 2, 7, 4096], P('pipe', None, None, 'dp')
- long_grad: float32 [4, 2, 256, 128], P('pipe', None, 'dp')
The draws below stay inside these ranges and needn't reach their ends.
All inputs are finite; a program needn't handle non-finite values.
Results may differ from the reference program's by a relative error of at most 0.0058.
Values may be sent and summed in bfloat16 or wider, within the bound.
A program may use at most 64 MiB of HBM per device.

```python
import jax
import jax.numpy as jnp
from jax import lax

C = 4096
K = 128
SHORT = 7
BLOCKS = 2
GROUPS = 256
SECTIONS = 4
SEQ = 1024


def levels(rng, dims, shards, low, largest):
    def one(dim, shards_of):
        heights = jax.random.uniform(jax.random.fold_in(jax.random.fold_in(rng, 6), dim), (shards_of,), jnp.float32, low / len(shards), largest / len(shards))
        return jnp.repeat(jnp.exp(heights), dims[dim] // shards_of).reshape((-1,) + (1,) * (len(dims) - dim - 1))

    gain = one(*shards[0])
    for cut in shards[1:]:
        gain = gain * one(*cut)
    return gain


def scatter_about(own_key, dims, scale, most, cuts=(), kind=jnp.bfloat16):
    values = jax.random.normal(own_key, dims, jnp.float32) * scale
    if len(cuts) > 0:
        values = levels(own_key, dims, cuts, -0.22, 0.18) * values
    return jnp.clip(values, min=-most, max=most).astype(kind)


def setup_inputs(seed: int = 0) -> dict:
    keys = jax.random.split(jax.random.key(seed), 5)
    return {
        "section_input": scatter_about(keys[0], (SECTIONS, SEQ, C), 1.0, 6.0, ((0, 4), (1, 8))),
        "out_grad": scatter_about(keys[1], (SECTIONS, SEQ, C), 1.0, 6.0, ((0, 4), (1, 8))),
        "short_filter": scatter_about(keys[2], (SECTIONS, BLOCKS, SHORT, C), SHORT ** -0.5, 2.0, ((0, 4), (3, 8))),
        "long_filter": scatter_about(keys[3], (SECTIONS, BLOCKS, GROUPS, K), K ** -0.5, 0.5, ((0, 4), (2, 8))),
    }


band_rows = 32


def band_tables(taps):
    band_count = taps // band_rows + 1
    first = jnp.arange(band_count, dtype=jnp.int32)[:, None, None] * band_rows
    row_pos = jnp.arange(band_rows, dtype=jnp.int32)[None, :, None]
    col_pos = jnp.arange(band_rows, dtype=jnp.int32)[None, None, :]
    lags = (first + row_pos - col_pos).reshape(-1)
    onehot = lags[:, None] == jnp.arange(taps, dtype=jnp.int32)[None, :]
    return onehot.astype(jnp.bfloat16).T, onehot.astype(jnp.float32)


def make_bands(filt, spread):
    groups = filt.shape[0]
    flat = jnp.dot(filt, spread, preferred_element_type=jnp.float32).astype(jnp.bfloat16)
    return flat.reshape(groups, -1, band_rows, band_rows).transpose(1, 0, 2, 3)


def as_blocks(field, groups):
    return field.reshape(-1, band_rows, groups, field.shape[1] // groups).astype(jnp.float32)


def causal_mix(padded, bands, block_count):
    band_count, groups = bands.shape[0], bands.shape[1]
    blocks = as_blocks(padded, groups)
    weights = bands.astype(jnp.float32)
    total = jnp.zeros((block_count, band_rows, groups, blocks.shape[3]), jnp.float32)
    for band in range(band_count):
        start = band_count - 1 - band
        total = total + jnp.einsum("gij,bjgc->bigc", weights[band], blocks[start:start + block_count])
    return total.reshape(block_count * band_rows, -1)


def anti_mix(padded, bands, block_count):
    band_count, groups = bands.shape[0], bands.shape[1]
    blocks = as_blocks(padded, groups)
    weights = bands.astype(jnp.float32)
    total = jnp.zeros((block_count, band_rows, groups, blocks.shape[3]), jnp.float32)
    for band in range(band_count):
        total = total + jnp.einsum("gij,bigc->bjgc", weights[band], blocks[band:band + block_count])
    return total.reshape(block_count * band_rows, -1)


def lag_past(grad, padded, collect, groups, band_count):
    grad_blocks = as_blocks(grad, groups)
    value_blocks = as_blocks(padded, groups)
    block_count = grad_blocks.shape[0]
    pieces = []
    for band in range(band_count):
        start = band_count - 1 - band
        pieces.append(jnp.einsum("bigc,bjgc->gij", grad_blocks, value_blocks[start:start + block_count]))
    stacked = jnp.stack(pieces, axis=1).reshape(groups, -1)
    return jnp.dot(stacked, collect, precision=lax.Precision.HIGHEST)


def short_mix(padded, taps_row, row_count):
    reach = taps_row.shape[0] - 1
    total = jnp.zeros((row_count, padded.shape[1]), jnp.float32)
    for tap_index in range(taps_row.shape[0]):
        start = reach - tap_index
        total = total + taps_row[tap_index].astype(jnp.float32) * padded[start:start + row_count].astype(jnp.float32)
    return total


def short_back(padded, taps_row, row_count):
    total = jnp.zeros((row_count, padded.shape[1]), jnp.float32)
    for tap_index in range(taps_row.shape[0]):
        total = total + taps_row[tap_index].astype(jnp.float32) * padded[tap_index:tap_index + row_count].astype(jnp.float32)
    return total


def short_corr(grad, padded, tap_count):
    reach = tap_count - 1
    row_count = grad.shape[0]
    grad_wide = grad.astype(jnp.float32)
    rows_out = []
    for tap_index in range(tap_count):
        start = reach - tap_index
        rows_out.append(jnp.sum(grad_wide * padded[start:start + row_count].astype(jnp.float32), axis=0))
    return jnp.stack(rows_out)


def section_backward(first_input, top_grad, short_all, long_all):
    seq_rows, width = first_input.shape
    groups, taps = long_all.shape[1], long_all.shape[2]
    tap_count = short_all.shape[1]
    reach = tap_count - 1
    band_count = taps // band_rows + 1
    spread, collect = band_tables(taps)
    block_count = seq_rows // band_rows
    first_bands = make_bands(long_all[0], spread)
    second_bands = make_bands(long_all[1], spread)
    tap_zeros = jnp.zeros((taps, width), jnp.bfloat16)
    reach_zeros = jnp.zeros((reach, width), jnp.bfloat16)
    input_past = jnp.concatenate([reach_zeros, first_input])
    mixed_one = short_mix(input_past, short_all[0], seq_rows).astype(jnp.bfloat16)
    mixed_one_past = jnp.concatenate([tap_zeros, mixed_one])
    long_one = causal_mix(mixed_one_past, first_bands, block_count)
    middle = (first_input.astype(jnp.float32) + long_one).astype(jnp.bfloat16)
    middle_past = jnp.concatenate([reach_zeros, middle])
    mixed_two = short_mix(middle_past, short_all[1], seq_rows).astype(jnp.bfloat16)
    grad_after = jnp.concatenate([top_grad, tap_zeros])
    dmix_two = anti_mix(grad_after, second_bands, block_count).astype(jnp.bfloat16)
    dlong_two = lag_past(top_grad, jnp.concatenate([tap_zeros, mixed_two]), collect, groups, band_count)
    back_two = short_back(jnp.concatenate([dmix_two, reach_zeros]), short_all[1], seq_rows)
    middle_grad = (top_grad.astype(jnp.float32) + back_two).astype(jnp.bfloat16)
    dshort_two = short_corr(dmix_two, middle_past, tap_count)
    middle_after = jnp.concatenate([middle_grad, tap_zeros])
    dmix_one = anti_mix(middle_after, first_bands, block_count).astype(jnp.bfloat16)
    dlong_one = lag_past(middle_grad, mixed_one_past, collect, groups, band_count)
    back_one = short_back(jnp.concatenate([dmix_one, reach_zeros]), short_all[0], seq_rows)
    input_grad = (middle_grad.astype(jnp.float32) + back_one).astype(jnp.bfloat16)
    dshort_one = short_corr(dmix_one, input_past, tap_count)
    return input_grad, jnp.stack([dshort_one, dshort_two]), jnp.stack([dlong_one, dlong_two])


def reference(section_input, out_grad, short_filter, long_filter):
    def one_section(index):
        return section_backward(section_input[index], out_grad[index], short_filter[index], long_filter[index])

    input_grad, short_grad, long_grad = lax.map(one_section, jnp.arange(SECTIONS, dtype=jnp.int32))
    passed_grad = jnp.concatenate([input_grad[1:], jnp.zeros_like(input_grad[:1])], axis=0)
    factor = float(SEQ) ** -0.5
    return passed_grad, short_grad * factor, long_grad * factor
```

```python
import functools

import jax
import jax.numpy as jnp
from jax import lax
from jax.experimental import pallas as pl
from jax.experimental.pallas import tpu as pltpu
from jax.sharding import PartitionSpec as P

MESH = pl.DeviceIdType.MESH
LANES = 128
PER_GROUP = 16
F32 = jnp.float32
BF16 = jnp.bfloat16
NT = (((1,), (1,)), ((), ()))
NN = (((1,), (0,)), ((), ()))
TN = (((0,), (0,)), ((), ()))


def mm(a, b, dims):
    return lax.dot_general(a, b, dims, preferred_element_type=F32)


def lanes_of(rows):
    return lax.broadcasted_iota(jnp.int32, (rows, LANES), 1)


def past_block(x):
    return jnp.concatenate([jnp.zeros((PER_GROUP, LANES), x.dtype), x[:-PER_GROUP]], axis=0)


def next_block(x):
    return jnp.concatenate([x[PER_GROUP:], jnp.zeros((PER_GROUP, LANES), x.dtype)], axis=0)


def shift_past(x, k):
    if k == 0:
        return x
    rolled = pltpu.roll(x, k, 1)
    return jnp.where(lanes_of(x.shape[0]) < k, past_block(rolled), rolled)


def shift_next(x, k):
    if k == 0:
        return x
    rolled = pltpu.roll(x, LANES - k, 1)
    return jnp.where(lanes_of(x.shape[0]) < LANES - k, rolled, next_block(rolled))


def kernel(n, pipes, chunks, tap_count, batch, factor,
           x_ref, g_ref, sf_ref, lf_ref,
           out_ref, short_ref, long_ref,
           recv, xt, ot, obuf, zbuf, wide, now_ref, past_ref, corr, lag,
           send_sem, recv_sem, local_sem, osend_sem, orecv_sem, zero_sem):
    stage = lax.axis_index("pipe")
    me = lax.axis_index("dp")
    rows = x_ref.shape[0]
    width = chunks * LANES
    per_chunk = LANES // PER_GROUP
    groups = chunks * per_chunk

    barrier = pltpu.get_barrier_semaphore()
    for j in range(1, n):
        pl.semaphore_signal(barrier, inc=1, device_id=(stage, lax.rem(me + j, n)), device_id_type=MESH)

    @pl.when(stage < pipes - 1)
    def _():
        for j in range(n):
            pl.semaphore_signal(barrier, inc=1, device_id=(stage + 1, j), device_id_type=MESH)

    pl.semaphore_wait(barrier, n - 1 + n * jnp.minimum(stage, 1))

    def columns(device, q):
        return pl.ds(pl.multiple_of(device * width + q * LANES, LANES), LANES)

    def in_copy(a, q, j, slot):
        to = lax.rem(me + j, n)
        return pltpu.make_async_remote_copy(
            src_ref=(x_ref, g_ref)[a].at[:, columns(to, q)],
            dst_ref=recv.at[a, q, slot],
            send_sem=send_sem.at[a, q, j],
            recv_sem=recv_sem.at[a, q, j],
            device_id=(stage, to),
            device_id_type=MESH,
        )

    def own_copy(a, q):
        return pltpu.make_async_copy(
            (x_ref, g_ref)[a].at[:, columns(me, q)], recv.at[a, q, me], local_sem.at[a, q]
        )

    def out_copy(q, j, source):
        to = lax.rem(me + j, n)
        return pltpu.make_async_remote_copy(
            src_ref=obuf.at[q, to],
            dst_ref=out_ref.at[:, columns(source, q)],
            send_sem=osend_sem.at[q, j],
            recv_sem=orecv_sem.at[q, j],
            device_id=(stage - 1, to),
            device_id_type=MESH,
        )

    @pl.loop(0, chunks)
    def _(q):
        for j in range(1, n):
            for a in range(2):
                in_copy(a, q, j, me).start()
        for a in range(2):
            own_copy(a, q).start()

    zero_copy = pltpu.make_async_copy(zbuf, out_ref, zero_sem)

    @pl.when(stage == pipes - 1)
    def _():
        zbuf[...] = jnp.zeros_like(zbuf)
        zero_copy.start()

    square = (LANES, LANES)
    row_pos = lax.broadcasted_iota(jnp.int32, square, 0)
    col_pos = lax.broadcasted_iota(jnp.int32, square, 1)
    eye = (row_pos == col_pos).astype(BF16)
    upper = row_pos <= col_pos

    @pl.loop(0, chunks)
    def _(q):
        for blk in range(2):
            taps_q = sf_ref[blk, :, pl.ds(pl.multiple_of(q * LANES, LANES), LANES)]
            for k in range(tap_count):
                spread = jnp.broadcast_to(taps_q[k:k + 1].astype(F32), square).astype(BF16)
                wide[q, blk * tap_count + k] = mm(eye, spread, NT)

    @pl.loop(0, groups)
    def _(g):
        for blk in range(2):
            filt = lf_ref[blk, pl.ds(g, 1)]
            circ = pltpu.roll(jnp.broadcast_to(filt, square), 0, 1, stride=1, stride_axis=0)
            now_ref[blk, g] = jnp.where(upper, circ, 0.0).astype(BF16)
            past_ref[blk, g] = jnp.where(upper, 0.0, circ).astype(BF16)

    def causal(v, blk, g):
        return mm(
            jnp.concatenate([v, past_block(v)], axis=1),
            jnp.concatenate([now_ref[blk, g], past_ref[blk, g]], axis=0), NN,
        )

    def anti(v, blk, g):
        return mm(
            jnp.concatenate([v, next_block(v)], axis=1),
            jnp.concatenate([now_ref[blk, g], past_ref[blk, g]], axis=1), NT,
        )

    def lag_part(values, grad, blk, g):
        pairs = mm(values, jnp.concatenate([grad, next_block(grad)], axis=1), TN)
        joined = jnp.where(upper, pairs[:, :LANES], pairs[:, LANES:])
        total = joined[:8]
        for i in range(1, LANES // 8):
            total = total + pltpu.roll(joined[8 * i:8 * i + 8], LANES - 8 * i, 1)
        lag[pl.ds(pl.multiple_of((blk * groups + g) * 8, 8), 8)] = total

    def tap(q, gl, blk, k):
        one = wide[q, blk * tap_count + k, pl.ds(pl.multiple_of(gl * PER_GROUP, PER_GROUP), PER_GROUP)]
        return jnp.concatenate([one] * n, axis=0)

    def short_mix(x, q, gl, blk):
        total = tap(q, gl, blk, 0) * x
        for k in range(1, tap_count):
            total = total + tap(q, gl, blk, k) * shift_past(x, k)
        return total.astype(BF16)

    def short_back(base, d, x, q, gl, blk):
        total = base
        at = pl.ds(pl.multiple_of(gl * PER_GROUP, PER_GROUP), PER_GROUP)
        for k in range(tap_count):
            moved = shift_next(d, k)
            total = total + tap(q, gl, blk, k) * moved
            prod = moved * x
            part = prod[:PER_GROUP]
            for b in range(1, n):
                part = part + prod[b * PER_GROUP:(b + 1) * PER_GROUP]
            corr[blk * tap_count + k, at] = part
        return total.astype(BF16)

    @pl.loop(0, chunks)
    def _(q):
        for j in range(1, n):
            for a in range(2):
                in_copy(a, q, j, lax.rem(me - j + n, n)).wait_recv()
        for a in range(2):
            own_copy(a, q).wait()
        for a in range(2):
            for b in range(n):
                turned = mm(eye, recv[a, q, b], NT).astype(BF16)
                xt[a, :, b * PER_GROUP:(b + 1) * PER_GROUP, :] = turned.reshape(
                    per_chunk, PER_GROUP, LANES
                )

        @pl.loop(0, per_chunk // batch)
        def _(step):
            local = [step * batch + u for u in range(batch)]
            every = range(batch)
            glob = [q * per_chunk + gl for gl in local]
            top = [xt[1, gl] for gl in local]
            src = [xt[0, gl].astype(F32) for gl in local]
            dmix_two = [anti(top[u], 1, glob[u]).astype(BF16).astype(F32) for u in every]
            mixed_one = [short_mix(src[u], q, local[u], 0) for u in every]
            long_one = [causal(mixed_one[u], 0, glob[u]) for u in every]
            middle = [(src[u] + long_one[u]).astype(BF16).astype(F32) for u in every]
            middle_grad = [
                short_back(top[u].astype(F32), dmix_two[u], middle[u], q, local[u], 1) for u in every
            ]
            dmix_one = [anti(middle_grad[u], 0, glob[u]).astype(BF16).astype(F32) for u in every]
            mixed_two = [short_mix(middle[u], q, local[u], 1) for u in every]
            for u in every:
                lag_part(mixed_two[u], top[u], 1, glob[u])
            for u in every:
                ot[local[u]] = short_back(
                    middle_grad[u].astype(F32), dmix_one[u], src[u], q, local[u], 0
                )
            for u in every:
                lag_part(mixed_one[u], middle_grad[u], 0, glob[u])

        @pl.when(stage > 0)
        def _():
            for b in range(n):
                piece = ot[:, b * PER_GROUP:(b + 1) * PER_GROUP, :].reshape(square)
                obuf[q, b] = mm(eye, piece, NT).astype(BF16)
            for j in range(n):
                out_copy(q, j, me).start()

        ones = jnp.ones((8, 2 * LANES), BF16)
        for blk in range(2):
            for k in range(tap_count):
                part = corr[blk * tap_count + k]
                high = part.astype(BF16)
                low = (part - high.astype(F32)).astype(BF16)
                summed = mm(ones, jnp.concatenate([high, low], axis=1), NT)
                short_ref[blk, k:k + 1, pl.ds(pl.multiple_of(q * LANES, LANES), LANES)] = (
                    summed[:1] * factor
                )

    total = lag[pl.ds(0, 2 * groups, stride=8), :]
    for r in range(1, 8):
        total = total + pltpu.roll(lag[pl.ds(r, 2 * groups, stride=8), :], LANES - r, 1)
    total = total * factor
    long_ref[0] = total[:groups]
    long_ref[1] = total[groups:]

    @pl.loop(0, chunks)
    def _(q):
        for j in range(1, n):
            for a in range(2):
                in_copy(a, q, j, me).wait_send()

    @pl.when(stage == pipes - 1)
    def _():
        zero_copy.wait()

    @pl.when(stage > 0)
    def _():
        @pl.loop(0, chunks)
        def _(q):
            for j in range(n):
                out_copy(q, j, me).wait_send()

    @pl.when(stage < pipes - 1)
    def _():
        @pl.loop(0, chunks)
        def _(q):
            for j in range(n):
                out_copy(q, j, lax.rem(me - j + n, n)).wait_recv()


def body(n, pipes, section_input, out_grad, short_filter, long_filter):
    rows, channels = section_input.shape[1:]
    tap_count = short_filter.shape[2]
    groups, taps = long_filter.shape[2:]
    width = channels // n
    chunks = width // LANES
    assert rows == LANES and taps == LANES and width == groups * PER_GROUP
    per_chunk = LANES // PER_GROUP
    batch = max(1, min(4, 32 // n))
    factor = float(rows * n) ** (-0.5)
    vmem = pl.BlockSpec(memory_space=pltpu.VMEM)
    anywhere = pl.BlockSpec(memory_space=pl.ANY)
    dma = pltpu.SemaphoreType.DMA
    passed, short_grad, long_grad = pl.pallas_call(
        functools.partial(kernel, n, pipes, chunks, tap_count, batch, factor),
        out_shape=(
            jax.ShapeDtypeStruct((rows, channels), BF16),
            jax.ShapeDtypeStruct((2, tap_count, width), F32),
            jax.ShapeDtypeStruct((2, groups, taps), F32),
        ),
        in_specs=[anywhere, anywhere, vmem, vmem],
        out_specs=(anywhere, vmem, vmem),
        scratch_shapes=[
            pltpu.VMEM((2, chunks, n, LANES, LANES), BF16),
            pltpu.VMEM((2, per_chunk, n * PER_GROUP, LANES), BF16),
            pltpu.VMEM((per_chunk, n * PER_GROUP, LANES), BF16),
            pltpu.VMEM((chunks, n, LANES, LANES), BF16),
            pltpu.VMEM((rows, channels), BF16),
            pltpu.VMEM((chunks, 2 * tap_count, LANES, LANES), F32),
            pltpu.VMEM((2, groups, LANES, LANES), BF16),
            pltpu.VMEM((2, groups, LANES, LANES), BF16),
            pltpu.VMEM((2 * tap_count, LANES, LANES), F32),
            pltpu.VMEM((2 * groups * 8, LANES), F32),
            dma((2, chunks, n)),
            dma((2, chunks, n)),
            dma((2, chunks)),
            dma((chunks, n)),
            dma((chunks, n)),
            dma(()),
        ],
        compiler_params=pltpu.CompilerParams(
            collective_id=0, has_side_effects=True, vmem_limit_bytes=48 * 1024 * 1024
        ),
    )(section_input[0], out_grad[0], short_filter[0], long_filter[0].astype(F32))
    return passed[None], short_grad[None], long_grad[None]


def solution(mesh):
    in_specs = (
        P("pipe", "dp", None),
        P("pipe", "dp", None),
        P("pipe", None, None, "dp"),
        P("pipe", None, "dp", None),
    )
    out_specs = (P("pipe", "dp", None), P("pipe", None, None, "dp"), P("pipe", None, "dp", None))
    run = functools.partial(body, mesh.shape["dp"], mesh.shape["pipe"])
    return jax.shard_map(run, mesh=mesh, in_specs=in_specs, out_specs=out_specs, check_vma=False)
```

```python
import functools

import jax
import jax.numpy as jnp
from jax import lax
from jax.experimental import pallas as pl
from jax.experimental.pallas import tpu as pltpu
from jax.sharding import PartitionSpec as P

MESH = pl.DeviceIdType.MESH
LANES = 128
PER_GROUP = 16
F32 = jnp.float32
BF16 = jnp.bfloat16
NT = (((1,), (1,)), ((), ()))
NN = (((1,), (0,)), ((), ()))
TN = (((0,), (0,)), ((), ()))


def mm(a, b, dims):
    return lax.dot_general(a, b, dims, preferred_element_type=F32)


def lanes_of(rows):
    return lax.broadcasted_iota(jnp.int32, (rows, LANES), 1)


def past_block(x):
    return jnp.concatenate([jnp.zeros((PER_GROUP, LANES), x.dtype), x[:-PER_GROUP]], axis=0)


def next_block(x):
    return jnp.concatenate([x[PER_GROUP:], jnp.zeros((PER_GROUP, LANES), x.dtype)], axis=0)


def shift_past(x, k):
    if k == 0:
        return x
    rolled = pltpu.roll(x, k, 1)
    return jnp.where(lanes_of(x.shape[0]) < k, past_block(rolled), rolled)


def shift_next(x, k):
    if k == 0:
        return x
    rolled = pltpu.roll(x, LANES - k, 1)
    return jnp.where(lanes_of(x.shape[0]) < LANES - k, rolled, next_block(rolled))


def flip(index, mask):
    out = index
    bit = 1
    while bit <= mask:
        if mask & bit:
            out = out + bit - 2 * bit * lax.rem(lax.div(index, bit), 2)
        bit *= 2
    return out


def orders(n):
    far = list(range(1, n // 2))
    later = far[1:] + far[:1]
    even = [2 * m for m in far] + [2 * m + 1 for m in far]
    odd = [2 * m for m in later] + [2 * m + 1 for m in later]
    return list(zip(even + [1], odd + [1]))


def kernel(n, pipes, chunks, tap_count, batch, factor,
           x_ref, g_ref, sf_ref, lf_ref,
           out_ref, short_ref, long_ref,
           recv, xt, ot, obuf, zbuf, wide, now_ref, past_ref, corr, lag, lf_wide,
           send_sem, recv_sem, local_sem, osend_sem, orecv_sem, zero_sem):
    stage = lax.axis_index("pipe")
    me = lax.axis_index("dp")
    rows = x_ref.shape[0]
    width = chunks * LANES
    per_chunk = LANES // PER_GROUP
    groups = chunks * per_chunk

    barrier = pltpu.get_barrier_semaphore()
    for j in range(1, n):
        pl.semaphore_signal(barrier, inc=1, device_id=(stage, lax.rem(me + j, n)), device_id_type=MESH)

    @pl.when(stage < pipes - 1)
    def _():
        for j in range(n):
            pl.semaphore_signal(barrier, inc=1, device_id=(stage + 1, j), device_id_type=MESH)

    pl.semaphore_wait(barrier, n - 1 + n * jnp.minimum(stage, 1))

    def columns(device, q):
        return pl.ds(pl.multiple_of(device * width + q * LANES, LANES), LANES)

    core = lax.rem(me, 2)

    def pick(step):
        first, second = step
        return (
            first + core * (second - first),
            flip(me, first) + core * (flip(me, second) - flip(me, first)),
        )

    def in_copy(a, q, j, to, slot):
        return pltpu.make_async_remote_copy(
            src_ref=(x_ref, g_ref)[a].at[:, columns(to, q)],
            dst_ref=recv.at[a, q, slot],
            send_sem=send_sem.at[a, q, j],
            recv_sem=recv_sem.at[a, q, j],
            device_id=(stage, to),
            device_id_type=MESH,
        )

    def own_copy(a, q):
        return pltpu.make_async_copy(
            (x_ref, g_ref)[a].at[:, columns(me, q)], recv.at[a, q, me], local_sem.at[a, q]
        )

    def out_copy(q, j, to, source):
        return pltpu.make_async_remote_copy(
            src_ref=obuf.at[q, to],
            dst_ref=out_ref.at[:, columns(source, q)],
            send_sem=osend_sem.at[q, j],
            recv_sem=orecv_sem.at[q, j],
            device_id=(stage - 1, to),
            device_id_type=MESH,
        )

    @pl.loop(0, chunks)
    def _(q):
        for step in orders(n):
            for a in range(2):
                in_copy(a, q, *pick(step), me).start()
        for a in range(2):
            own_copy(a, q).start()

    zero_copy = pltpu.make_async_copy(zbuf, out_ref, zero_sem)

    @pl.when(stage == pipes - 1)
    def _():
        zbuf[...] = jnp.zeros_like(zbuf)
        zero_copy.start()

    square = (LANES, LANES)
    row_pos = lax.broadcasted_iota(jnp.int32, square, 0)
    col_pos = lax.broadcasted_iota(jnp.int32, square, 1)
    eye = (row_pos == col_pos).astype(BF16)
    upper = row_pos <= col_pos

    @pl.loop(0, chunks)
    def _(q):
        for blk in range(2):
            taps_q = sf_ref[:, blk, pl.ds(pl.multiple_of(q * LANES, LANES), LANES)]
            for k in range(tap_count):
                spread = jnp.broadcast_to(taps_q[k:k + 1].astype(F32), square).astype(BF16)
                wide[q, blk * tap_count + k] = mm(eye, spread, NT)

    lf_wide[...] = lf_ref[...].astype(F32)

    @pl.loop(0, groups)
    def _(g):
        for blk in range(2):
            filt = lf_wide[blk, pl.ds(g, 1)]
            circ = pltpu.roll(jnp.broadcast_to(filt, square), 0, 1, stride=1, stride_axis=0)
            now_ref[blk, g] = jnp.where(upper, circ, 0.0).astype(BF16)
            past_ref[blk, g] = jnp.where(upper, 0.0, circ).astype(BF16)

    def causal(v, blk, g):
        return mm(
            jnp.concatenate([v, past_block(v)], axis=1),
            jnp.concatenate([now_ref[blk, g], past_ref[blk, g]], axis=0), NN,
        )

    def anti(v, blk, g):
        return mm(
            jnp.concatenate([v, next_block(v)], axis=1),
            jnp.concatenate([now_ref[blk, g], past_ref[blk, g]], axis=1), NT,
        )

    def lag_part(values, grad, blk, g):
        pairs = mm(values, jnp.concatenate([grad, next_block(grad)], axis=1), TN)
        joined = jnp.where(upper, pairs[:, :LANES], pairs[:, LANES:])
        total = joined[:8]
        for i in range(1, LANES // 8):
            total = total + pltpu.roll(joined[8 * i:8 * i + 8], LANES - 8 * i, 1)
        lag[pl.ds(pl.multiple_of((blk * groups + g) * 8, 8), 8)] = total

    def tap(q, gl, blk, k):
        one = wide[q, blk * tap_count + k, pl.ds(pl.multiple_of(gl * PER_GROUP, PER_GROUP), PER_GROUP)]
        return jnp.concatenate([one] * n, axis=0)

    def short_mix(x, q, gl, blk):
        total = tap(q, gl, blk, 0) * x
        for k in range(1, tap_count):
            total = total + tap(q, gl, blk, k) * shift_past(x, k)
        return total.astype(BF16)

    def short_back(base, d, x, q, gl, blk):
        total = base
        at = pl.ds(pl.multiple_of(gl * PER_GROUP, PER_GROUP), PER_GROUP)
        for k in range(tap_count):
            moved = shift_next(d, k)
            total = total + tap(q, gl, blk, k) * moved
            prod = moved * x
            part = prod[:PER_GROUP]
            for b in range(1, n):
                part = part + prod[b * PER_GROUP:(b + 1) * PER_GROUP]
            corr[blk * tap_count + k, at] = part
        return total.astype(BF16)

    @pl.loop(0, chunks)
    def _(q):
        for j in range(1, n):
            for a in range(2):
                in_copy(a, q, j, flip(me, j), flip(me, j)).wait_recv()
        for a in range(2):
            own_copy(a, q).wait()
        for a in range(2):
            for b in range(n):
                turned = mm(eye, recv[a, q, b], NT).astype(BF16)
                xt[a, :, b * PER_GROUP:(b + 1) * PER_GROUP, :] = turned.reshape(
                    per_chunk, PER_GROUP, LANES
                )

        @pl.loop(0, per_chunk // batch)
        def _(step):
            local = [step * batch + u for u in range(batch)]
            every = range(batch)
            glob = [q * per_chunk + gl for gl in local]
            top = [xt[1, gl] for gl in local]
            src = [xt[0, gl].astype(F32) for gl in local]
            dmix_two = [anti(top[u], 1, glob[u]).astype(BF16).astype(F32) for u in every]
            mixed_one = [short_mix(src[u], q, local[u], 0) for u in every]
            long_one = [causal(mixed_one[u], 0, glob[u]) for u in every]
            middle = [(src[u] + long_one[u]).astype(BF16).astype(F32) for u in every]
            middle_grad = [
                short_back(top[u].astype(F32), dmix_two[u], middle[u], q, local[u], 1) for u in every
            ]
            dmix_one = [anti(middle_grad[u], 0, glob[u]).astype(BF16).astype(F32) for u in every]
            mixed_two = [short_mix(middle[u], q, local[u], 1) for u in every]
            for u in every:
                lag_part(mixed_two[u], top[u], 1, glob[u])
            for u in every:
                ot[local[u]] = short_back(
                    middle_grad[u].astype(F32), dmix_one[u], src[u], q, local[u], 0
                )
            for u in every:
                lag_part(mixed_one[u], middle_grad[u], 0, glob[u])

        @pl.when(stage > 0)
        def _():
            for b in range(n):
                piece = ot[:, b * PER_GROUP:(b + 1) * PER_GROUP, :].reshape(square)
                obuf[q, b] = mm(eye, piece, NT).astype(BF16)
            for step in orders(n) + [(0, 0)]:
                out_copy(q, *pick(step), me).start()

        ones = jnp.ones((8, 2 * LANES), BF16)
        for blk in range(2):
            for k in range(tap_count):
                part = corr[blk * tap_count + k]
                high = part.astype(BF16)
                low = (part - high.astype(F32)).astype(BF16)
                summed = mm(ones, jnp.concatenate([high, low], axis=1), NT)
                short_ref[k, blk:blk + 1, pl.ds(pl.multiple_of(q * LANES, LANES), LANES)] = (
                    summed[:1] * factor
                )

    total = lag[pl.ds(0, 2 * groups, stride=8), :]
    for r in range(1, 8):
        total = total + pltpu.roll(lag[pl.ds(r, 2 * groups, stride=8), :], LANES - r, 1)
    total = total * factor
    long_ref[0] = total[:groups]
    long_ref[1] = total[groups:]

    @pl.loop(0, chunks)
    def _(q):
        for j in range(1, n):
            for a in range(2):
                in_copy(a, q, j, flip(me, j), me).wait_send()

    @pl.when(stage == pipes - 1)
    def _():
        zero_copy.wait()

    @pl.when(stage > 0)
    def _():
        @pl.loop(0, chunks)
        def _(q):
            for j in range(n):
                out_copy(q, j, flip(me, j), me).wait_send()

    @pl.when(stage < pipes - 1)
    def _():
        @pl.loop(0, chunks)
        def _(q):
            for j in range(n):
                out_copy(q, j, flip(me, j), flip(me, j)).wait_recv()


def body(n, pipes, section_input, out_grad, short_filter, long_filter):
    rows, channels = section_input.shape[1:]
    tap_count = short_filter.shape[2]
    groups, taps = long_filter.shape[2:]
    width = channels // n
    chunks = width // LANES
    assert rows == LANES and taps == LANES and width == groups * PER_GROUP
    per_chunk = LANES // PER_GROUP
    batch = max(1, min(4, 32 // n))
    factor = float(rows * n) ** (-0.5)
    vmem = pl.BlockSpec(memory_space=pltpu.VMEM)
    anywhere = pl.BlockSpec(memory_space=pltpu.HBM)
    dma = pltpu.SemaphoreType.DMA
    passed, short_grad, long_grad = pl.pallas_call(
        functools.partial(kernel, n, pipes, chunks, tap_count, batch, factor),
        out_shape=(
            jax.ShapeDtypeStruct((rows, channels), BF16),
            jax.ShapeDtypeStruct((tap_count, 2, width), F32),
            jax.ShapeDtypeStruct((2, groups, taps), F32),
        ),
        in_specs=[anywhere, anywhere, vmem, vmem],
        out_specs=(anywhere, vmem, vmem),
        scratch_shapes=[
            pltpu.VMEM((2, chunks, n, LANES, LANES), BF16),
            pltpu.VMEM((2, per_chunk, n * PER_GROUP, LANES), BF16),
            pltpu.VMEM((per_chunk, n * PER_GROUP, LANES), BF16),
            pltpu.VMEM((chunks, n, LANES, LANES), BF16),
            pltpu.VMEM((rows, channels), BF16),
            pltpu.VMEM((chunks, 2 * tap_count, LANES, LANES), F32),
            pltpu.VMEM((2, groups, LANES, LANES), BF16),
            pltpu.VMEM((2, groups, LANES, LANES), BF16),
            pltpu.VMEM((2 * tap_count, LANES, LANES), F32),
            pltpu.VMEM((2 * groups * 8, LANES), F32),
            pltpu.VMEM((2, groups, LANES), F32),
            dma((2, chunks, n)),
            dma((2, chunks, n)),
            dma((2, chunks)),
            dma((chunks, n)),
            dma((chunks, n)),
            dma(()),
        ],
        compiler_params=pltpu.CompilerParams(
            collective_id=0, has_side_effects=True, vmem_limit_bytes=63 * 1024 * 1024
        ),
    )(section_input[0], out_grad[0], short_filter[0].transpose(1, 0, 2), long_filter[0])
    return passed[None], short_grad.transpose(1, 0, 2)[None], long_grad[None]


def solution(mesh):
    in_specs = (
        P("pipe", "dp", None),
        P("pipe", "dp", None),
        P("pipe", None, None, "dp"),
        P("pipe", None, "dp", None),
    )
    out_specs = (P("pipe", "dp", None), P("pipe", None, None, "dp"), P("pipe", None, "dp", None))
    run = functools.partial(body, mesh.shape["dp"], mesh.shape["pipe"])
    return jax.shard_map(run, mesh=mesh, in_specs=in_specs, out_specs=out_specs, check_vma=False)
```

```python
import functools

import jax
import jax.numpy as jnp
from jax import lax
from jax.experimental import pallas as pl
from jax.experimental.pallas import tpu as pltpu
from jax.sharding import PartitionSpec as P

MESH = pl.DeviceIdType.MESH
LANES = 128
PER_GROUP = 16
F32 = jnp.float32
BF16 = jnp.bfloat16
NT = (((1,), (1,)), ((), ()))
NN = (((1,), (0,)), ((), ()))
TN = (((0,), (0,)), ((), ()))


def mm(a, b, dims):
    return lax.dot_general(a, b, dims, preferred_element_type=F32)


def lanes_of(rows):
    return lax.broadcasted_iota(jnp.int32, (rows, LANES), 1)


def past_block(x):
    return jnp.concatenate([jnp.zeros((PER_GROUP, LANES), x.dtype), x[:-PER_GROUP]], axis=0)


def next_block(x):
    return jnp.concatenate([x[PER_GROUP:], jnp.zeros((PER_GROUP, LANES), x.dtype)], axis=0)


def shift_past(x, k):
    if k == 0:
        return x
    rolled = pltpu.roll(x, k, 1)
    return jnp.where(lanes_of(x.shape[0]) < k, past_block(rolled), rolled)


def shift_next(x, k):
    if k == 0:
        return x
    rolled = pltpu.roll(x, LANES - k, 1)
    return jnp.where(lanes_of(x.shape[0]) < LANES - k, rolled, next_block(rolled))


def flip(index, mask):
    out = index
    bit = 1
    while bit <= mask:
        if mask & bit:
            out = out + bit - 2 * bit * lax.rem(lax.div(index, bit), 2)
        bit *= 2
    return out


def orders(n):
    far = list(range(1, n // 2))
    later = far[1:] + far[:1]
    even = [2 * m for m in far] + [2 * m + 1 for m in far]
    odd = [2 * m for m in later] + [2 * m + 1 for m in later]
    return list(zip(even + [1], odd + [1]))


def kernel(n, pipes, chunks, tap_count, batch, factor,
           x_ref, g_ref, sf_ref, lf_ref,
           out_ref, short_ref, long_ref,
           recv, xt, ot, obuf, wide, now_ref, past_ref, corr, lag, lf_wide, mix_ref, back_ref,
           send_sem, recv_sem, local_sem, osend_sem, orecv_sem):
    stage = lax.axis_index("pipe")
    me = lax.axis_index("dp")
    rows = x_ref.shape[0]
    width = chunks * LANES
    per_chunk = LANES // PER_GROUP
    groups = chunks * per_chunk

    barrier = pltpu.get_barrier_semaphore()
    for j in range(1, n):
        pl.semaphore_signal(barrier, inc=1, device_id=(stage, lax.rem(me + j, n)), device_id_type=MESH)

    @pl.when(stage < pipes - 1)
    def _():
        for j in range(n):
            pl.semaphore_signal(barrier, inc=1, device_id=(stage + 1, j), device_id_type=MESH)

    pl.semaphore_wait(barrier, n - 1 + n * jnp.minimum(stage, 1))

    def columns(device, q):
        return pl.ds(pl.multiple_of(device * width + q * LANES, LANES), LANES)

    core = lax.rem(me, 2)

    def pick(step):
        first, second = step
        return (
            first + core * (second - first),
            flip(me, first) + core * (flip(me, second) - flip(me, first)),
        )

    def in_copy(a, q, j, to, slot):
        return pltpu.make_async_remote_copy(
            src_ref=(x_ref, g_ref)[a].at[:, columns(to, q)],
            dst_ref=recv.at[a, q, slot],
            send_sem=send_sem.at[a, q, j],
            recv_sem=recv_sem.at[a, q, j],
            device_id=(stage, to),
            device_id_type=MESH,
        )

    def own_copy(a, q):
        return pltpu.make_async_copy(
            (x_ref, g_ref)[a].at[:, columns(me, q)], recv.at[a, q, me], local_sem.at[a, q]
        )

    def out_copy(q, j, to, source):
        return pltpu.make_async_remote_copy(
            src_ref=obuf.at[q, to],
            dst_ref=out_ref.at[:, columns(source, q)],
            send_sem=osend_sem.at[q, j],
            recv_sem=orecv_sem.at[q, j],
            device_id=(stage - 1, to),
            device_id_type=MESH,
        )

    @pl.loop(0, chunks)
    def _(q):
        for step in orders(n):
            for a in range(2):
                in_copy(a, q, *pick(step), me).start()
        for a in range(2):
            own_copy(a, q).start()

    square = (LANES, LANES)
    row_pos = lax.broadcasted_iota(jnp.int32, square, 0)
    col_pos = lax.broadcasted_iota(jnp.int32, square, 1)
    eye = (row_pos == col_pos).astype(BF16)
    upper = row_pos <= col_pos

    @pl.loop(0, chunks)
    def _(q):
        for blk in range(2):
            taps_q = sf_ref[:, blk, pl.ds(pl.multiple_of(q * LANES, LANES), LANES)]
            for k in range(tap_count):
                spread = jnp.broadcast_to(taps_q[k:k + 1].astype(F32), square).astype(BF16)
                wide[q, blk * tap_count + k] = mm(eye, spread, NT).astype(BF16)

    wide_row = lax.broadcasted_iota(jnp.int32, (LANES, 2 * LANES), 0)
    wide_col = lax.broadcasted_iota(jnp.int32, (LANES, 2 * LANES), 1)
    for k in range(tap_count):
        at = pl.ds(k * LANES, LANES)
        mix_ref[at] = (wide_col == wide_row + k).astype(BF16)
        away = jnp.where(wide_col < LANES, wide_col + k, wide_col - 2 * LANES + k)
        back_ref[at] = (wide_row == away).astype(BF16)
    fold_row = lax.broadcasted_iota(jnp.int32, (PER_GROUP, n * PER_GROUP), 0)
    fold_col = lax.broadcasted_iota(jnp.int32, (PER_GROUP, n * PER_GROUP), 1)
    fold = (lax.rem(fold_col, PER_GROUP) == fold_row).astype(BF16)

    lf_wide[...] = lf_ref[...].astype(F32)

    @pl.loop(0, groups)
    def _(g):
        for blk in range(2):
            filt = lf_wide[blk, pl.ds(g, 1)]
            circ = pltpu.roll(jnp.broadcast_to(filt, square), 0, 1, stride=1, stride_axis=0)
            now_ref[blk, g] = jnp.where(upper, circ, 0.0).astype(BF16)
            past_ref[blk, g] = jnp.where(upper, 0.0, circ).astype(BF16)

    def causal(v, blk, g):
        return mm(
            jnp.concatenate([v, past_block(v)], axis=1),
            jnp.concatenate([now_ref[blk, g], past_ref[blk, g]], axis=0), NN,
        )

    def anti(v, blk, g):
        return mm(
            jnp.concatenate([v, next_block(v)], axis=1),
            jnp.concatenate([now_ref[blk, g], past_ref[blk, g]], axis=1), NT,
        )

    def lag_part(values, grad, blk, g):
        pairs = mm(values, jnp.concatenate([grad, next_block(grad)], axis=1), TN)
        joined = jnp.where(upper, pairs[:, :LANES], pairs[:, LANES:])
        total = joined[:8]
        for i in range(1, LANES // 8):
            total = total + pltpu.roll(joined[8 * i:8 * i + 8], LANES - 8 * i, 1)
        lag[pl.ds(pl.multiple_of((blk * groups + g) * 8, 8), 8)] = total

    def tap(q, gl, blk, k):
        one = wide[q, blk * tap_count + k, pl.ds(pl.multiple_of(gl * PER_GROUP, PER_GROUP), PER_GROUP)]
        return jnp.concatenate([one] * n, axis=0)

    def weighted(x, q, gl, blk):
        return jnp.concatenate([tap(q, gl, blk, k) * x for k in range(tap_count)], axis=1)

    def short_mix(xs, q, local, blk):
        terms = jnp.concatenate([weighted(x, q, gl, blk) for x, gl in zip(xs, local)], axis=0)
        both = mm(terms, mix_ref[...], NN)
        size = n * PER_GROUP
        return [
            (both[u * size:(u + 1) * size, :LANES]
             + past_block(both[u * size:(u + 1) * size, LANES:])).astype(BF16)
            for u in range(len(xs))
        ]

    def short_back(bases, ds, q, local, blk):
        terms = jnp.concatenate([weighted(d, q, gl, blk) for d, gl in zip(ds, local)], axis=0)
        both = mm(terms, back_ref[...], NN)
        size = n * PER_GROUP
        return [
            (base.astype(F32) + both[u * size:(u + 1) * size, :LANES]
             + next_block(both[u * size:(u + 1) * size, LANES:])).astype(BF16)
            for u, base in enumerate(bases)
        ]

    def short_corr(d, x, gl, blk):
        at = pl.ds(pl.multiple_of(gl * PER_GROUP, PER_GROUP), PER_GROUP)
        prods = jnp.concatenate([shift_next(d, k) * x for k in range(tap_count)], axis=1)
        sums = mm(fold, prods, NN)
        for k in range(tap_count):
            corr[blk * tap_count + k, at] = sums[:, k * LANES:(k + 1) * LANES]

    @pl.loop(0, chunks)
    def _(q):
        for j in range(1, n):
            for a in range(2):
                in_copy(a, q, j, flip(me, j), flip(me, j)).wait_recv()
        for a in range(2):
            own_copy(a, q).wait()
        for a in range(2):
            for b in range(n):
                turned = mm(eye, recv[a, q, b], NT).astype(BF16)
                xt[a, :, b * PER_GROUP:(b + 1) * PER_GROUP, :] = turned.reshape(
                    per_chunk, PER_GROUP, LANES
                )

        @pl.loop(0, per_chunk // batch)
        def _(step):
            local = [step * batch + u for u in range(batch)]
            every = range(batch)
            glob = [q * per_chunk + gl for gl in local]
            top = [xt[1, gl] for gl in local]
            src = [xt[0, gl] for gl in local]
            dmix_two = [anti(top[u], 1, glob[u]).astype(BF16) for u in every]
            mixed_one = short_mix(src, q, local, 0)
            long_one = [causal(mixed_one[u], 0, glob[u]) for u in every]
            middle = [(src[u].astype(F32) + long_one[u]).astype(BF16) for u in every]
            middle_grad = short_back(top, dmix_two, q, local, 1)
            dmix_one = [anti(middle_grad[u], 0, glob[u]).astype(BF16) for u in every]
            mixed_two = short_mix(middle, q, local, 1)
            for u in every:
                short_corr(dmix_two[u], middle[u], local[u], 1)
            for u in every:
                lag_part(mixed_two[u], top[u], 1, glob[u])
            result = short_back(middle_grad, dmix_one, q, local, 0)
            for u in every:
                ot[local[u]] = result[u]
            for u in every:
                short_corr(dmix_one[u], src[u], local[u], 0)
            for u in every:
                lag_part(mixed_one[u], middle_grad[u], 0, glob[u])

        @pl.when(stage > 0)
        def _():
            for b in range(n):
                piece = ot[:, b * PER_GROUP:(b + 1) * PER_GROUP, :].reshape(square)
                obuf[q, b] = mm(eye, piece, NT).astype(BF16)
            for step in orders(n) + [(0, 0)]:
                out_copy(q, *pick(step), me).start()

        ones = jnp.ones((8, 2 * LANES), BF16)
        for blk in range(2):
            for k in range(tap_count):
                part = corr[blk * tap_count + k]
                high = part.astype(BF16)
                low = (part - high.astype(F32)).astype(BF16)
                summed = mm(ones, jnp.concatenate([high, low], axis=1), NT)
                short_ref[k, blk:blk + 1, pl.ds(pl.multiple_of(q * LANES, LANES), LANES)] = (
                    summed[:1] * factor
                )

    total = lag[pl.ds(0, 2 * groups, stride=8), :]
    for r in range(1, 8):
        total = total + pltpu.roll(lag[pl.ds(r, 2 * groups, stride=8), :], LANES - r, 1)
    total = total * factor
    long_ref[0] = total[:groups]
    long_ref[1] = total[groups:]

    @pl.loop(0, chunks)
    def _(q):
        for j in range(1, n):
            for a in range(2):
                in_copy(a, q, j, flip(me, j), me).wait_send()

    @pl.when(stage > 0)
    def _():
        @pl.loop(0, chunks)
        def _(q):
            for j in range(n):
                out_copy(q, j, flip(me, j), me).wait_send()

    @pl.when(stage < pipes - 1)
    def _():
        @pl.loop(0, chunks)
        def _(q):
            for j in range(n):
                out_copy(q, j, flip(me, j), flip(me, j)).wait_recv()


def body(n, pipes, section_input, out_grad, short_filter, long_filter):
    rows, channels = section_input.shape[1:]
    tap_count = short_filter.shape[2]
    groups, taps = long_filter.shape[2:]
    width = channels // n
    chunks = width // LANES
    assert rows == LANES and taps == LANES and width == groups * PER_GROUP
    per_chunk = LANES // PER_GROUP
    batch = max(1, min(4, 32 // n))
    factor = float(rows * n) ** (-0.5)
    vmem = pl.BlockSpec(memory_space=pltpu.VMEM)
    anywhere = pl.BlockSpec(memory_space=pltpu.HBM)
    dma = pltpu.SemaphoreType.DMA
    passed, short_grad, long_grad = pl.pallas_call(
        functools.partial(kernel, n, pipes, chunks, tap_count, batch, factor),
        out_shape=(
            jax.ShapeDtypeStruct((rows, channels), BF16),
            jax.ShapeDtypeStruct((tap_count, 2, width), F32),
            jax.ShapeDtypeStruct((2, groups, taps), F32),
        ),
        in_specs=[anywhere, anywhere, vmem, vmem],
        out_specs=(anywhere, vmem, vmem),
        scratch_shapes=[
            pltpu.VMEM((2, chunks, n, LANES, LANES), BF16),
            pltpu.VMEM((2, per_chunk, n * PER_GROUP, LANES), BF16),
            pltpu.VMEM((per_chunk, n * PER_GROUP, LANES), BF16),
            pltpu.VMEM((chunks, n, LANES, LANES), BF16),
            pltpu.VMEM((chunks, 2 * tap_count, LANES, LANES), BF16),
            pltpu.VMEM((2, groups, LANES, LANES), BF16),
            pltpu.VMEM((2, groups, LANES, LANES), BF16),
            pltpu.VMEM((2 * tap_count, LANES, LANES), F32),
            pltpu.VMEM((2 * groups * 8, LANES), F32),
            pltpu.VMEM((2, groups, LANES), F32),
            pltpu.VMEM((tap_count * LANES, 2 * LANES), BF16),
            pltpu.VMEM((tap_count * LANES, 2 * LANES), BF16),
            dma((2, chunks, n)),
            dma((2, chunks, n)),
            dma((2, chunks)),
            dma((chunks, n)),
            dma((chunks, n)),
        ],
        compiler_params=pltpu.CompilerParams(
            collective_id=0, has_side_effects=True, vmem_limit_bytes=63 * 1024 * 1024
        ),
    )(section_input[0], out_grad[0], short_filter[0].transpose(1, 0, 2), long_filter[0])
    passed = jnp.where(lax.axis_index("pipe") < pipes - 1, passed, jnp.zeros_like(passed))
    return passed[None], short_grad.transpose(1, 0, 2)[None], long_grad[None]


def solution(mesh):
    in_specs = (
        P("pipe", "dp", None),
        P("pipe", "dp", None),
        P("pipe", None, None, "dp"),
        P("pipe", None, "dp", None),
    )
    out_specs = (P("pipe", "dp", None), P("pipe", None, None, "dp"), P("pipe", None, "dp", None))
    run = functools.partial(body, mesh.shape["dp"], mesh.shape["pipe"])
    return jax.shard_map(run, mesh=mesh, in_specs=in_specs, out_specs=out_specs, check_vma=False)
```

```python
import functools

import jax
import jax.numpy as jnp
from jax import lax
from jax.experimental import pallas as pl
from jax.experimental.pallas import tpu as pltpu
from jax.sharding import PartitionSpec as P

MESH = pl.DeviceIdType.MESH
LANES = 128
PER_GROUP = 16
F32 = jnp.float32
BF16 = jnp.bfloat16
NT = (((1,), (1,)), ((), ()))
NN = (((1,), (0,)), ((), ()))
TN = (((0,), (0,)), ((), ()))


def mm(a, b, dims):
    return lax.dot_general(a, b, dims, preferred_element_type=F32)


def lanes_of(rows):
    return lax.broadcasted_iota(jnp.int32, (rows, LANES), 1)


def past_block(x):
    return jnp.concatenate([jnp.zeros((PER_GROUP, LANES), x.dtype), x[:-PER_GROUP]], axis=0)


def next_block(x):
    return jnp.concatenate([x[PER_GROUP:], jnp.zeros((PER_GROUP, LANES), x.dtype)], axis=0)


def shift_past(x, k):
    if k == 0:
        return x
    rolled = pltpu.roll(x, k, 1)
    return jnp.where(lanes_of(x.shape[0]) < k, past_block(rolled), rolled)


def shift_next(x, k):
    if k == 0:
        return x
    rolled = pltpu.roll(x, LANES - k, 1)
    return jnp.where(lanes_of(x.shape[0]) < LANES - k, rolled, next_block(rolled))


def flip(index, mask):
    out = index
    bit = 1
    while bit <= mask:
        if mask & bit:
            out = out + bit - 2 * bit * lax.rem(lax.div(index, bit), 2)
        bit *= 2
    return out


def orders(n):
    far = list(range(1, n // 2))
    later = far[1:] + far[:1]
    even = [2 * m for m in far] + [2 * m + 1 for m in far]
    odd = [2 * m for m in later] + [2 * m + 1 for m in later]
    return list(zip(even + [1], odd + [1]))


def kernel(n, pipes, chunks, tap_count, batch, factor,
           x_ref, g_ref, sf_ref, lf_ref,
           out_ref, short_ref, long_ref,
           recv, xt, ot, obuf, wide, now_ref, past_ref, corr, lag, lf_wide, mix_ref,
           send_sem, recv_sem, local_sem, osend_sem, orecv_sem):
    stage = lax.axis_index("pipe")
    me = lax.axis_index("dp")
    rows = x_ref.shape[0]
    width = chunks * LANES
    per_chunk = LANES // PER_GROUP
    groups = chunks * per_chunk

    barrier = pltpu.get_barrier_semaphore()
    for j in range(1, n):
        pl.semaphore_signal(barrier, inc=1, device_id=(stage, lax.rem(me + j, n)), device_id_type=MESH)

    @pl.when(stage < pipes - 1)
    def _():
        for j in range(n):
            pl.semaphore_signal(barrier, inc=1, device_id=(stage + 1, j), device_id_type=MESH)

    pl.semaphore_wait(barrier, n - 1 + n * jnp.minimum(stage, 1))

    def columns(device, q):
        return pl.ds(pl.multiple_of(device * width + q * LANES, LANES), LANES)

    core = lax.rem(me, 2)

    def pick(step):
        first, second = step
        return (
            first + core * (second - first),
            flip(me, first) + core * (flip(me, second) - flip(me, first)),
        )

    def in_copy(a, q, j, to, slot):
        return pltpu.make_async_remote_copy(
            src_ref=(x_ref, g_ref)[a].at[:, columns(to, q)],
            dst_ref=recv.at[a, q, slot],
            send_sem=send_sem.at[a, q, j],
            recv_sem=recv_sem.at[a, q, j],
            device_id=(stage, to),
            device_id_type=MESH,
        )

    def own_copy(a, q):
        return pltpu.make_async_copy(
            (x_ref, g_ref)[a].at[:, columns(me, q)], recv.at[a, q, me], local_sem.at[a, q]
        )

    def out_copy(q, j, to, source):
        return pltpu.make_async_remote_copy(
            src_ref=obuf.at[q, to],
            dst_ref=out_ref.at[:, columns(source, q)],
            send_sem=osend_sem.at[q, j],
            recv_sem=orecv_sem.at[q, j],
            device_id=(stage - 1, to),
            device_id_type=MESH,
        )

    @pl.loop(0, chunks)
    def _(q):
        for step in orders(n):
            for a in range(2):
                in_copy(a, q, *pick(step), me).start()
        for a in range(2):
            own_copy(a, q).start()

    square = (LANES, LANES)
    row_pos = lax.broadcasted_iota(jnp.int32, square, 0)
    col_pos = lax.broadcasted_iota(jnp.int32, square, 1)
    eye = (row_pos == col_pos).astype(BF16)
    upper = row_pos <= col_pos

    @pl.loop(0, chunks)
    def _(q):
        for blk in range(2):
            taps_q = sf_ref[:, blk, pl.ds(pl.multiple_of(q * LANES, LANES), LANES)]
            for k in range(tap_count):
                spread = jnp.broadcast_to(taps_q[k:k + 1].astype(F32), square).astype(BF16)
                wide[q, blk * tap_count + k] = mm(eye, spread, NT).astype(BF16)

    wide_row = lax.broadcasted_iota(jnp.int32, (LANES, 2 * LANES), 0)
    wide_col = lax.broadcasted_iota(jnp.int32, (LANES, 2 * LANES), 1)
    for k in range(tap_count):
        at = pl.ds(k * LANES, LANES)
        mix_ref[at] = (wide_col == wide_row + k).astype(BF16)
    fold_row = lax.broadcasted_iota(jnp.int32, (PER_GROUP, n * PER_GROUP), 0)
    fold_col = lax.broadcasted_iota(jnp.int32, (PER_GROUP, n * PER_GROUP), 1)
    fold = (lax.rem(fold_col, PER_GROUP) == fold_row).astype(BF16)

    lf_wide[...] = lf_ref[...].astype(F32)

    @pl.loop(0, groups)
    def _(g):
        for blk in range(2):
            filt = lf_wide[blk, pl.ds(g, 1)]
            circ = pltpu.roll(jnp.broadcast_to(filt, square), 0, 1, stride=1, stride_axis=0)
            now_ref[blk, g] = jnp.where(upper, circ, 0.0).astype(BF16)
            past_ref[blk, g] = jnp.where(upper, 0.0, circ).astype(BF16)

    def causal(v, blk, g):
        return mm(
            jnp.concatenate([v, past_block(v)], axis=1),
            jnp.concatenate([now_ref[blk, g], past_ref[blk, g]], axis=0), NN,
        )

    def anti(v, blk, g):
        return mm(
            jnp.concatenate([v, next_block(v)], axis=1),
            jnp.concatenate([now_ref[blk, g], past_ref[blk, g]], axis=1), NT,
        )

    def lag_part(values, grad, blk, g):
        pairs = mm(values, jnp.concatenate([grad, next_block(grad)], axis=1), TN)
        joined = jnp.where(upper, pairs[:, :LANES], pairs[:, LANES:])
        total = joined[:8]
        for i in range(1, LANES // 8):
            total = total + pltpu.roll(joined[8 * i:8 * i + 8], LANES - 8 * i, 1)
        lag[pl.ds(pl.multiple_of((blk * groups + g) * 8, 8), 8)] = total

    def tap(q, gl, blk, k):
        one = wide[q, blk * tap_count + k, pl.ds(pl.multiple_of(gl * PER_GROUP, PER_GROUP), PER_GROUP)]
        return jnp.concatenate([one] * n, axis=0)

    def weighted(x, q, gl, blk):
        return jnp.concatenate([tap(q, gl, blk, k) * x for k in range(tap_count)], axis=1)

    def short_mix(xs, q, local, blk):
        terms = jnp.concatenate([weighted(x, q, gl, blk) for x, gl in zip(xs, local)], axis=0)
        both = mm(terms, mix_ref[...], NN)
        size = n * PER_GROUP
        return [
            (both[u * size:(u + 1) * size, :LANES]
             + past_block(both[u * size:(u + 1) * size, LANES:])).astype(BF16)
            for u in range(len(xs))
        ]

    def short_back(base, d, x, q, gl, blk):
        at = pl.ds(pl.multiple_of(gl * PER_GROUP, PER_GROUP), PER_GROUP)
        moved = [shift_next(d, k) for k in range(tap_count)]
        total = base.astype(F32)
        for k in range(tap_count):
            total = total + tap(q, gl, blk, k).astype(F32) * moved[k].astype(F32)
        sums = mm(fold, jnp.concatenate([m * x for m in moved], axis=1), NN)
        for k in range(tap_count):
            corr[blk * tap_count + k, at] = sums[:, k * LANES:(k + 1) * LANES]
        return total.astype(BF16)

    @pl.loop(0, chunks)
    def _(q):
        for j in range(1, n):
            for a in range(2):
                in_copy(a, q, j, flip(me, j), flip(me, j)).wait_recv()
        for a in range(2):
            own_copy(a, q).wait()
        for a in range(2):
            for b in range(n):
                turned = mm(eye, recv[a, q, b], NT).astype(BF16)
                xt[a, :, b * PER_GROUP:(b + 1) * PER_GROUP, :] = turned.reshape(
                    per_chunk, PER_GROUP, LANES
                )

        @pl.loop(0, per_chunk // batch)
        def _(step):
            local = [step * batch + u for u in range(batch)]
            every = range(batch)
            glob = [q * per_chunk + gl for gl in local]
            top = [xt[1, gl] for gl in local]
            src = [xt[0, gl] for gl in local]
            dmix_two = [anti(top[u], 1, glob[u]).astype(BF16) for u in every]
            mixed_one = short_mix(src, q, local, 0)
            long_one = [causal(mixed_one[u], 0, glob[u]) for u in every]
            middle = [(src[u].astype(F32) + long_one[u]).astype(BF16) for u in every]
            middle_grad = [
                short_back(top[u], dmix_two[u], middle[u], q, local[u], 1) for u in every
            ]
            dmix_one = [anti(middle_grad[u], 0, glob[u]).astype(BF16) for u in every]
            mixed_two = short_mix(middle, q, local, 1)
            for u in every:
                lag_part(mixed_two[u], top[u], 1, glob[u])
            for u in every:
                ot[local[u]] = short_back(middle_grad[u], dmix_one[u], src[u], q, local[u], 0)
            for u in every:
                lag_part(mixed_one[u], middle_grad[u], 0, glob[u])

        @pl.when(stage > 0)
        def _():
            for b in range(n):
                piece = ot[:, b * PER_GROUP:(b + 1) * PER_GROUP, :].reshape(square)
                obuf[q, b] = mm(eye, piece, NT).astype(BF16)
            for step in orders(n) + [(0, 0)]:
                out_copy(q, *pick(step), me).start()

        ones = jnp.ones((8, 2 * LANES), BF16)
        for blk in range(2):
            for k in range(tap_count):
                part = corr[blk * tap_count + k]
                high = part.astype(BF16)
                low = (part - high.astype(F32)).astype(BF16)
                summed = mm(ones, jnp.concatenate([high, low], axis=1), NT)
                short_ref[k, blk:blk + 1, pl.ds(pl.multiple_of(q * LANES, LANES), LANES)] = (
                    summed[:1] * factor
                )

    total = lag[pl.ds(0, 2 * groups, stride=8), :]
    for r in range(1, 8):
        total = total + pltpu.roll(lag[pl.ds(r, 2 * groups, stride=8), :], LANES - r, 1)
    total = total * factor
    long_ref[0] = total[:groups]
    long_ref[1] = total[groups:]

    @pl.loop(0, chunks)
    def _(q):
        for j in range(1, n):
            for a in range(2):
                in_copy(a, q, j, flip(me, j), me).wait_send()

    @pl.when(stage > 0)
    def _():
        @pl.loop(0, chunks)
        def _(q):
            for j in range(n):
                out_copy(q, j, flip(me, j), me).wait_send()

    @pl.when(stage < pipes - 1)
    def _():
        @pl.loop(0, chunks)
        def _(q):
            for j in range(n):
                out_copy(q, j, flip(me, j), flip(me, j)).wait_recv()


def finish(pipes, passed_ref, short_ref, long_ref, out_ref, short_out, long_out, zeros, sem, sem_s, sem_l):
    stage = lax.axis_index("pipe")
    parts = sem.shape[0]
    size = passed_ref.shape[0] // parts
    small = [
        pltpu.make_async_copy(short_ref, short_out, sem_s),
        pltpu.make_async_copy(long_ref, long_out, sem_l),
    ]
    for copy in small:
        copy.start()

    def move(source):
        copies = [
            pltpu.make_async_copy(
                source.at[pl.ds(i * size, size)], out_ref.at[pl.ds(i * size, size)], sem.at[i]
            )
            for i in range(parts)
        ]
        for copy in copies:
            copy.start()
        for copy in copies:
            copy.wait()

    @pl.when(stage < pipes - 1)
    def _():
        move(passed_ref)

    @pl.when(stage == pipes - 1)
    def _():
        zeros[...] = jnp.zeros_like(zeros)
        move(zeros)

    for copy in small:
        copy.wait()


def body(n, pipes, section_input, out_grad, short_filter, long_filter):
    rows, channels = section_input.shape[1:]
    tap_count = short_filter.shape[2]
    groups, taps = long_filter.shape[2:]
    width = channels // n
    chunks = width // LANES
    assert rows == LANES and taps == LANES and width == groups * PER_GROUP
    per_chunk = LANES // PER_GROUP
    batch = max(1, min(8, 64 // n))
    factor = float(rows * n) ** (-0.5)
    vmem = pl.BlockSpec(memory_space=pltpu.VMEM)
    anywhere = pl.BlockSpec(memory_space=pltpu.HBM)
    dma = pltpu.SemaphoreType.DMA
    passed, short_grad, long_grad = pl.pallas_call(
        functools.partial(kernel, n, pipes, chunks, tap_count, batch, factor),
        out_shape=(
            jax.ShapeDtypeStruct((rows, channels), BF16),
            jax.ShapeDtypeStruct((tap_count, 2, width), F32),
            jax.ShapeDtypeStruct((2, groups, taps), F32),
        ),
        in_specs=[anywhere, anywhere, vmem, vmem],
        out_specs=(anywhere, vmem, vmem),
        scratch_shapes=[
            pltpu.VMEM((2, chunks, n, LANES, LANES), BF16),
            pltpu.VMEM((2, per_chunk, n * PER_GROUP, LANES), BF16),
            pltpu.VMEM((per_chunk, n * PER_GROUP, LANES), BF16),
            pltpu.VMEM((chunks, n, LANES, LANES), BF16),
            pltpu.VMEM((chunks, 2 * tap_count, LANES, LANES), BF16),
            pltpu.VMEM((2, groups, LANES, LANES), BF16),
            pltpu.VMEM((2, groups, LANES, LANES), BF16),
            pltpu.VMEM((2 * tap_count, LANES, LANES), F32),
            pltpu.VMEM((2 * groups * 8, LANES), F32),
            pltpu.VMEM((2, groups, LANES), F32),
            pltpu.VMEM((tap_count * LANES, 2 * LANES), BF16),
            dma((2, chunks, n)),
            dma((2, chunks, n)),
            dma((2, chunks)),
            dma((chunks, n)),
            dma((chunks, n)),
        ],
        compiler_params=pltpu.CompilerParams(
            collective_id=0, has_side_effects=True, vmem_limit_bytes=63 * 1024 * 1024
        ),
    )(section_input[0], out_grad[0], short_filter[0].transpose(1, 0, 2), long_filter[0])
    passed, short_grad, long_grad = pl.pallas_call(
        functools.partial(finish, pipes),
        out_shape=tuple(jax.ShapeDtypeStruct(x.shape, x.dtype) for x in (passed, short_grad, long_grad)),
        in_specs=[anywhere] * 3,
        out_specs=(anywhere,) * 3,
        scratch_shapes=[pltpu.VMEM((rows, channels), BF16), dma((8,)), dma(()), dma(())],
        compiler_params=pltpu.CompilerParams(vmem_limit_bytes=63 * 1024 * 1024),
    )(passed, short_grad, long_grad)
    return passed[None], short_grad.transpose(1, 0, 2)[None], long_grad[None]


def solution(mesh):
    in_specs = (
        P("pipe", "dp", None),
        P("pipe", "dp", None),
        P("pipe", None, None, "dp"),
        P("pipe", None, "dp", None),
    )
    out_specs = (P("pipe", "dp", None), P("pipe", None, None, "dp"), P("pipe", None, "dp", None))
    run = functools.partial(body, mesh.shape["dp"], mesh.shape["pipe"])
    return jax.shard_map(run, mesh=mesh, in_specs=in_specs, out_specs=out_specs, check_vma=False)
```

```python
import functools

import jax
import jax.numpy as jnp
from jax import lax
from jax.experimental import pallas as pl
from jax.experimental.pallas import tpu as pltpu
from jax.sharding import PartitionSpec as P

MESH = pl.DeviceIdType.MESH
LANES = 128
PER_GROUP = 16
F32 = jnp.float32
BF16 = jnp.bfloat16
NT = (((1,), (1,)), ((), ()))
NN = (((1,), (0,)), ((), ()))
TN = (((0,), (0,)), ((), ()))


def mm(a, b, dims):
    return lax.dot_general(a, b, dims, preferred_element_type=F32)


def lanes_of(rows):
    return lax.broadcasted_iota(jnp.int32, (rows, LANES), 1)


def past_block(x):
    return jnp.concatenate([jnp.zeros((PER_GROUP, LANES), x.dtype), x[:-PER_GROUP]], axis=0)


def next_block(x):
    return jnp.concatenate([x[PER_GROUP:], jnp.zeros((PER_GROUP, LANES), x.dtype)], axis=0)


def shift_past(x, k):
    if k == 0:
        return x
    rolled = pltpu.roll(x, k, 1)
    return jnp.where(lanes_of(x.shape[0]) < k, past_block(rolled), rolled)


def shift_next(x, k):
    if k == 0:
        return x
    rolled = pltpu.roll(x, LANES - k, 1)
    return jnp.where(lanes_of(x.shape[0]) < LANES - k, rolled, next_block(rolled))


def flip(index, mask):
    out = index
    bit = 1
    while bit <= mask:
        if mask & bit:
            out = out + bit - 2 * bit * lax.rem(lax.div(index, bit), 2)
        bit *= 2
    return out


def orders(n):
    far = list(range(1, n // 2))
    later = far[1:] + far[:1]
    even = [2 * m for m in far] + [2 * m + 1 for m in far]
    odd = [2 * m for m in later] + [2 * m + 1 for m in later]
    return list(zip(even + [1], odd + [1]))


def kernel(n, pipes, chunks, tap_count, batch, factor,
           x_ref, g_ref, sf_ref, lf_ref,
           out_ref, short_ref, long_ref,
           recv, sbuf, xt, ot, obuf, wide, now_ref, past_ref, corr, lag, lf_wide,
           send_sem, recv_sem, stage_sem, local_sem, osend_sem, orecv_sem):
    stage = lax.axis_index("pipe")
    me = lax.axis_index("dp")
    rows = x_ref.shape[0]
    width = chunks * LANES
    per_chunk = LANES // PER_GROUP
    groups = chunks * per_chunk

    def columns(device, q):
        return pl.ds(pl.multiple_of(device * width + q * LANES, LANES), LANES)

    core = lax.rem(me, 2)

    def pick(step):
        first, second = step
        return (
            first + core * (second - first),
            flip(me, first) + core * (flip(me, second) - flip(me, first)),
        )

    def in_copy(a, q, j, to, slot):
        return pltpu.make_async_remote_copy(
            src_ref=sbuf.at[a, q, j],
            dst_ref=recv.at[a, q, slot],
            send_sem=send_sem.at[a, q, j],
            recv_sem=recv_sem.at[a, q, j],
            device_id=(stage, to),
            device_id_type=MESH,
        )

    def stage_copy(a, q, j, to):
        return pltpu.make_async_copy(
            (x_ref, g_ref)[a].at[:, columns(to, q)], sbuf.at[a, q, j], stage_sem.at[a, q, j]
        )

    def own_copy(a, q):
        return pltpu.make_async_copy(
            (x_ref, g_ref)[a].at[:, columns(me, q)], recv.at[a, q, me], local_sem.at[a, q]
        )

    def out_copy(q, j, to, source):
        return pltpu.make_async_remote_copy(
            src_ref=obuf.at[q, to],
            dst_ref=out_ref.at[source, q],
            send_sem=osend_sem.at[q, j],
            recv_sem=orecv_sem.at[q, j],
            device_id=(stage - 1, to),
            device_id_type=MESH,
        )

    @pl.loop(0, chunks)
    def _(q):
        for step in orders(n):
            for a in range(2):
                stage_copy(a, q, *pick(step)).start()
        for a in range(2):
            own_copy(a, q).start()

    barrier = pltpu.get_barrier_semaphore()
    for j in range(1, n):
        pl.semaphore_signal(barrier, inc=1, device_id=(stage, lax.rem(me + j, n)), device_id_type=MESH)

    @pl.when(stage < pipes - 1)
    def _():
        for j in range(n):
            pl.semaphore_signal(barrier, inc=1, device_id=(stage + 1, j), device_id_type=MESH)

    pl.semaphore_wait(barrier, n - 1 + n * jnp.minimum(stage, 1))

    @pl.loop(0, chunks)
    def _(q):
        for step in orders(n):
            for a in range(2):
                stage_copy(a, q, *pick(step)).wait()
                in_copy(a, q, *pick(step), me).start()

    square = (LANES, LANES)
    row_pos = lax.broadcasted_iota(jnp.int32, square, 0)
    col_pos = lax.broadcasted_iota(jnp.int32, square, 1)
    eye = (row_pos == col_pos).astype(BF16)
    upper = row_pos <= col_pos

    @pl.loop(0, chunks)
    def _(q):
        for blk in range(2):
            taps_q = sf_ref[:, blk, pl.ds(pl.multiple_of(q * LANES, LANES), LANES)]
            for k in range(tap_count):
                spread = jnp.broadcast_to(taps_q[k:k + 1].astype(F32), square).astype(BF16)
                wide[q, blk * tap_count + k] = mm(eye, spread, NT).astype(BF16)

    fold_row = lax.broadcasted_iota(jnp.int32, (PER_GROUP, n * PER_GROUP), 0)
    fold_col = lax.broadcasted_iota(jnp.int32, (PER_GROUP, n * PER_GROUP), 1)
    fold = (lax.rem(fold_col, PER_GROUP) == fold_row).astype(BF16)

    lf_wide[...] = lf_ref[...].astype(F32)

    @pl.loop(0, groups)
    def _(g):
        for blk in range(2):
            filt = lf_wide[blk, pl.ds(g, 1)]
            circ = pltpu.roll(jnp.broadcast_to(filt, square), 0, 1, stride=1, stride_axis=0)
            now_ref[blk, g] = jnp.where(upper, circ, 0.0).astype(BF16)
            past_ref[blk, g] = jnp.where(upper, 0.0, circ).astype(BF16)

    def causal(v, blk, g):
        return mm(
            jnp.concatenate([v, past_block(v)], axis=1),
            jnp.concatenate([now_ref[blk, g], past_ref[blk, g]], axis=0), NN,
        )

    def anti(v, blk, g):
        return mm(
            jnp.concatenate([v, next_block(v)], axis=1),
            jnp.concatenate([now_ref[blk, g], past_ref[blk, g]], axis=1), NT,
        )

    def lag_part(values, grad, blk, g):
        pairs = mm(values, jnp.concatenate([grad, next_block(grad)], axis=1), TN)
        joined = jnp.where(upper, pairs[:, :LANES], pairs[:, LANES:])
        total = joined[:8]
        for i in range(1, LANES // 8):
            total = total + pltpu.roll(joined[8 * i:8 * i + 8], LANES - 8 * i, 1)
        lag[pl.ds(pl.multiple_of((blk * groups + g) * 8, 8), 8)] = total

    def tap(q, gl, blk, k):
        one = wide[q, blk * tap_count + k, pl.ds(pl.multiple_of(gl * PER_GROUP, PER_GROUP), PER_GROUP)]
        return jnp.concatenate([one] * n, axis=0)

    def short_mix(x, q, gl, blk):
        total = tap(q, gl, blk, 0).astype(F32) * x.astype(F32)
        for k in range(1, tap_count):
            total = total + tap(q, gl, blk, k).astype(F32) * shift_past(x, k).astype(F32)
        return total.astype(BF16)

    def short_back(base, d, x, q, gl, blk):
        at = pl.ds(pl.multiple_of(gl * PER_GROUP, PER_GROUP), PER_GROUP)
        moved = [shift_next(d, k) for k in range(tap_count)]
        total = base.astype(F32)
        for k in range(tap_count):
            total = total + tap(q, gl, blk, k).astype(F32) * moved[k].astype(F32)
        sums = mm(fold, jnp.concatenate([m * x for m in moved], axis=1), NN)
        for k in range(tap_count):
            corr[blk * tap_count + k, at] = sums[:, k * LANES:(k + 1) * LANES]
        return total.astype(BF16)

    @pl.loop(0, chunks)
    def _(q):
        for j in range(1, n):
            for a in range(2):
                in_copy(a, q, j, flip(me, j), flip(me, j)).wait_recv()
        for a in range(2):
            own_copy(a, q).wait()
        for a in range(2):
            for b in range(n):
                turned = mm(eye, recv[a, q, b], NT).astype(BF16)
                xt[a, :, b * PER_GROUP:(b + 1) * PER_GROUP, :] = turned.reshape(
                    per_chunk, PER_GROUP, LANES
                )

        @pl.loop(0, per_chunk // batch)
        def _(step):
            local = [step * batch + u for u in range(batch)]
            every = range(batch)
            glob = [q * per_chunk + gl for gl in local]
            top = [xt[1, gl] for gl in local]
            src = [xt[0, gl] for gl in local]
            dmix_two = [anti(top[u], 1, glob[u]).astype(BF16) for u in every]
            mixed_one = [short_mix(src[u], q, local[u], 0) for u in every]
            long_one = [causal(mixed_one[u], 0, glob[u]) for u in every]
            middle = [(src[u].astype(F32) + long_one[u]).astype(BF16) for u in every]
            middle_grad = [
                short_back(top[u], dmix_two[u], middle[u], q, local[u], 1) for u in every
            ]
            dmix_one = [anti(middle_grad[u], 0, glob[u]).astype(BF16) for u in every]
            mixed_two = [short_mix(middle[u], q, local[u], 1) for u in every]
            for u in every:
                lag_part(mixed_two[u], top[u], 1, glob[u])
            for u in every:
                ot[local[u]] = short_back(middle_grad[u], dmix_one[u], src[u], q, local[u], 0)
            for u in every:
                lag_part(mixed_one[u], middle_grad[u], 0, glob[u])

        @pl.when(stage > 0)
        def _():
            for b in range(n):
                piece = ot[:, b * PER_GROUP:(b + 1) * PER_GROUP, :].reshape(square)
                obuf[q, b] = mm(eye, piece, NT).astype(BF16)
            for step in orders(n) + [(0, 0)]:
                out_copy(q, *pick(step), me).start()

        ones = jnp.ones((8, 2 * LANES), BF16)
        for blk in range(2):
            for k in range(tap_count):
                part = corr[blk * tap_count + k]
                high = part.astype(BF16)
                low = (part - high.astype(F32)).astype(BF16)
                summed = mm(ones, jnp.concatenate([high, low], axis=1), NT)
                short_ref[k, blk:blk + 1, pl.ds(pl.multiple_of(q * LANES, LANES), LANES)] = (
                    summed[:1] * factor
                )

    total = lag[pl.ds(0, 2 * groups, stride=8), :]
    for r in range(1, 8):
        total = total + pltpu.roll(lag[pl.ds(r, 2 * groups, stride=8), :], LANES - r, 1)
    total = total * factor
    long_ref[0] = total[:groups]
    long_ref[1] = total[groups:]

    @pl.loop(0, chunks)
    def _(q):
        for j in range(1, n):
            for a in range(2):
                in_copy(a, q, j, flip(me, j), me).wait_send()

    @pl.when(stage > 0)
    def _():
        @pl.loop(0, chunks)
        def _(q):
            for j in range(n):
                out_copy(q, j, flip(me, j), me).wait_send()

    @pl.when(stage < pipes - 1)
    def _():
        @pl.loop(0, chunks)
        def _(q):
            for j in range(n):
                out_copy(q, j, flip(me, j), flip(me, j)).wait_recv()


def finish(pipes, parts_ref, short_ref, long_ref, out_ref, short_out, long_out, rows_ref, in_sem, out_sem):
    stage = lax.axis_index("pipe")
    n, chunks = parts_ref.shape[:2]
    width = chunks * LANES

    def columns(source):
        return pl.ds(source * width, width)

    def load(source, q):
        return pltpu.make_async_copy(
            parts_ref.at[source, q],
            rows_ref.at[:, pl.ds(source * width + q * LANES, LANES)],
            in_sem.at[source, q],
        )

    def store(source):
        return pltpu.make_async_copy(
            rows_ref.at[:, columns(source)], out_ref.at[:, columns(source)], out_sem.at[source]
        )

    @pl.when(stage < pipes - 1)
    def _():
        for source in range(n):
            for q in range(chunks):
                load(source, q).start()
        for source in range(n):
            for q in range(chunks):
                load(source, q).wait()
            store(source).start()

    @pl.when(stage == pipes - 1)
    def _():
        rows_ref[...] = jnp.zeros_like(rows_ref)
        for source in range(n):
            store(source).start()

    short_out[...] = short_ref[...]
    long_out[...] = long_ref[...]
    for source in range(n):
        store(source).wait()


def body(n, pipes, section_input, out_grad, short_filter, long_filter):
    rows, channels = section_input.shape[1:]
    tap_count = short_filter.shape[2]
    groups, taps = long_filter.shape[2:]
    width = channels // n
    chunks = width // LANES
    assert rows == LANES and taps == LANES and width == groups * PER_GROUP
    per_chunk = LANES // PER_GROUP
    batch = max(1, min(8, 64 // n))
    factor = float(rows * n) ** (-0.5)
    vmem = pl.BlockSpec(memory_space=pltpu.VMEM)
    anywhere = pl.BlockSpec(memory_space=pltpu.HBM)
    dma = pltpu.SemaphoreType.DMA
    parts, short_grad, long_grad = pl.pallas_call(
        functools.partial(kernel, n, pipes, chunks, tap_count, batch, factor),
        out_shape=(
            jax.ShapeDtypeStruct((n, chunks, LANES, LANES), BF16),
            jax.ShapeDtypeStruct((tap_count, 2, width), F32),
            jax.ShapeDtypeStruct((2, groups, taps), F32),
        ),
        in_specs=[anywhere, anywhere, vmem, vmem],
        out_specs=(anywhere, vmem, vmem),
        scratch_shapes=[
            pltpu.VMEM((2, chunks, n, LANES, LANES), BF16),
            pltpu.VMEM((2, chunks, n, LANES, LANES), BF16),
            pltpu.VMEM((2, per_chunk, n * PER_GROUP, LANES), BF16),
            pltpu.VMEM((per_chunk, n * PER_GROUP, LANES), BF16),
            pltpu.VMEM((chunks, n, LANES, LANES), BF16),
            pltpu.VMEM((chunks, 2 * tap_count, LANES, LANES), BF16),
            pltpu.VMEM((2, groups, LANES, LANES), BF16),
            pltpu.VMEM((2, groups, LANES, LANES), BF16),
            pltpu.VMEM((2 * tap_count, LANES, LANES), F32),
            pltpu.VMEM((2 * groups * 8, LANES), F32),
            pltpu.VMEM((2, groups, LANES), F32),
            dma((2, chunks, n)),
            dma((2, chunks, n)),
            dma((2, chunks, n)),
            dma((2, chunks)),
            dma((chunks, n)),
            dma((chunks, n)),
        ],
        compiler_params=pltpu.CompilerParams(
            collective_id=0, has_side_effects=True, vmem_limit_bytes=63 * 1024 * 1024
        ),
    )(section_input[0], out_grad[0], short_filter[0].transpose(1, 0, 2), long_filter[0])
    passed, short_grad, long_grad = pl.pallas_call(
        functools.partial(finish, pipes),
        out_shape=(
            jax.ShapeDtypeStruct((rows, channels), BF16),
            jax.ShapeDtypeStruct(short_grad.shape, F32),
            jax.ShapeDtypeStruct(long_grad.shape, F32),
        ),
        in_specs=[anywhere, vmem, vmem],
        out_specs=(anywhere, vmem, vmem),
        scratch_shapes=[pltpu.VMEM((rows, channels), BF16), dma((n, chunks)), dma((n,))],
        compiler_params=pltpu.CompilerParams(vmem_limit_bytes=63 * 1024 * 1024),
    )(parts, short_grad, long_grad)
    return passed[None], short_grad.transpose(1, 0, 2)[None], long_grad[None]


def solution(mesh):
    in_specs = (
        P("pipe", "dp", None),
        P("pipe", "dp", None),
        P("pipe", None, None, "dp"),
        P("pipe", None, "dp", None),
    )
    out_specs = (P("pipe", "dp", None), P("pipe", None, None, "dp"), P("pipe", None, "dp", None))
    run = functools.partial(body, mesh.shape["dp"], mesh.shape["pipe"])
    return jax.shard_map(run, mesh=mesh, in_specs=in_specs, out_specs=out_specs, check_vma=False)
```

```python
import functools

import jax
import jax.numpy as jnp
from jax import lax
from jax.experimental import pallas as pl
from jax.experimental.pallas import tpu as pltpu
from jax.sharding import PartitionSpec as P

MESH = pl.DeviceIdType.MESH
LANES = 128
PER_GROUP = 16
F32 = jnp.float32
BF16 = jnp.bfloat16
NT = (((1,), (1,)), ((), ()))
NN = (((1,), (0,)), ((), ()))
TN = (((0,), (0,)), ((), ()))


def mm(a, b, dims):
    return lax.dot_general(a, b, dims, preferred_element_type=F32)


def lanes_of(rows):
    return lax.broadcasted_iota(jnp.int32, (rows, LANES), 1)


def past_block(x):
    return jnp.concatenate([jnp.zeros((PER_GROUP, LANES), x.dtype), x[:-PER_GROUP]], axis=0)


def next_block(x):
    return jnp.concatenate([x[PER_GROUP:], jnp.zeros((PER_GROUP, LANES), x.dtype)], axis=0)


def shift_past(x, k):
    if k == 0:
        return x
    rolled = pltpu.roll(x, k, 1)
    return jnp.where(lanes_of(x.shape[0]) < k, past_block(rolled), rolled)


def shift_next(x, k):
    if k == 0:
        return x
    rolled = pltpu.roll(x, LANES - k, 1)
    return jnp.where(lanes_of(x.shape[0]) < LANES - k, rolled, next_block(rolled))


def flip(index, mask):
    out = index
    bit = 1
    while bit <= mask:
        if mask & bit:
            out = out + bit - 2 * bit * lax.rem(lax.div(index, bit), 2)
        bit *= 2
    return out


def orders(n):
    far = list(range(1, n // 2))
    later = far[1:] + far[:1]
    even = [2 * m for m in far] + [2 * m + 1 for m in far]
    odd = [2 * m for m in later] + [2 * m + 1 for m in later]
    return list(zip(even + [1], odd + [1]))


def kernel(n, pipes, chunks, tap_count, batch, factor,
           x_ref, g_ref, sf_ref, lf_ref,
           out_ref, short_ref, long_ref,
           recv, sbuf, xt, ot, obuf, wide, now_ref, past_ref, corr, lag, lf_wide,
           send_sem, recv_sem, stage_sem, local_sem, osend_sem, orecv_sem):
    stage = lax.axis_index("pipe")
    me = lax.axis_index("dp")
    rows = x_ref.shape[0]
    width = chunks * LANES
    per_chunk = LANES // PER_GROUP
    groups = chunks * per_chunk

    def columns(device, q):
        return pl.ds(pl.multiple_of(device * width + q * LANES, LANES), LANES)

    core = lax.rem(me, 2)

    def pick(step):
        first, second = step
        return (
            first + core * (second - first),
            flip(me, first) + core * (flip(me, second) - flip(me, first)),
        )

    def in_copy(a, q, j, to, slot):
        return pltpu.make_async_remote_copy(
            src_ref=sbuf.at[a, q, j],
            dst_ref=recv.at[a, q, slot],
            send_sem=send_sem.at[a, q, j],
            recv_sem=recv_sem.at[a, q, j],
            device_id=(stage, to),
            device_id_type=MESH,
        )

    def stage_copy(a, q, j, to):
        return pltpu.make_async_copy(
            (x_ref, g_ref)[a].at[:, columns(to, q)], sbuf.at[a, q, j], stage_sem.at[a, q, j]
        )

    def own_copy(a, q):
        return pltpu.make_async_copy(
            (x_ref, g_ref)[a].at[:, columns(me, q)], recv.at[a, q, me], local_sem.at[a, q]
        )

    def out_copy(q, j, to, source):
        return pltpu.make_async_remote_copy(
            src_ref=obuf.at[q, to],
            dst_ref=out_ref.at[:, columns(source, q)],
            send_sem=osend_sem.at[q, j],
            recv_sem=orecv_sem.at[q, j],
            device_id=(stage - 1, to),
            device_id_type=MESH,
        )

    @pl.loop(0, chunks)
    def _(q):
        for step in orders(n):
            for a in range(2):
                stage_copy(a, q, *pick(step)).start()
        for a in range(2):
            own_copy(a, q).start()

    barrier = pltpu.get_barrier_semaphore()
    for j in range(1, n):
        pl.semaphore_signal(barrier, inc=1, device_id=(stage, lax.rem(me + j, n)), device_id_type=MESH)

    @pl.when(stage < pipes - 1)
    def _():
        for j in range(n):
            pl.semaphore_signal(barrier, inc=1, device_id=(stage + 1, j), device_id_type=MESH)

    pl.semaphore_wait(barrier, n - 1 + n * jnp.minimum(stage, 1))

    @pl.loop(0, chunks)
    def _(q):
        for step in orders(n):
            for a in range(2):
                stage_copy(a, q, *pick(step)).wait()
                in_copy(a, q, *pick(step), me).start()

    square = (LANES, LANES)
    row_pos = lax.broadcasted_iota(jnp.int32, square, 0)
    col_pos = lax.broadcasted_iota(jnp.int32, square, 1)
    eye = (row_pos == col_pos).astype(BF16)
    upper = row_pos <= col_pos

    @pl.loop(0, chunks)
    def _(q):
        for blk in range(2):
            taps_q = sf_ref[:, blk, pl.ds(pl.multiple_of(q * LANES, LANES), LANES)]
            for k in range(tap_count):
                spread = jnp.broadcast_to(taps_q[k:k + 1].astype(F32), square).astype(BF16)
                wide[q, blk * tap_count + k] = mm(eye, spread, NT).astype(BF16)

    fold_row = lax.broadcasted_iota(jnp.int32, (PER_GROUP, n * PER_GROUP), 0)
    fold_col = lax.broadcasted_iota(jnp.int32, (PER_GROUP, n * PER_GROUP), 1)
    fold = (lax.rem(fold_col, PER_GROUP) == fold_row).astype(BF16)

    lf_wide[...] = lf_ref[...].astype(F32)

    @pl.loop(0, groups)
    def _(g):
        for blk in range(2):
            filt = lf_wide[blk, pl.ds(g, 1)]
            circ = pltpu.roll(jnp.broadcast_to(filt, square), 0, 1, stride=1, stride_axis=0)
            now_ref[blk, g] = jnp.where(upper, circ, 0.0).astype(BF16)
            past_ref[blk, g] = jnp.where(upper, 0.0, circ).astype(BF16)

    hold = min(1, chunks - 1)

    def arrive(q):
        for j in range(1, n):
            for a in range(2):
                in_copy(a, q, j, flip(me, j), flip(me, j)).wait_recv()
        for a in range(2):
            own_copy(a, q).wait()

    def send_far(q):
        for step in orders(n)[:-1]:
            out_copy(q, *pick(step), me).start()

    def causal(v, blk, g):
        return mm(
            jnp.concatenate([v, past_block(v)], axis=1),
            jnp.concatenate([now_ref[blk, g], past_ref[blk, g]], axis=0), NN,
        )

    def anti(v, blk, g):
        return mm(
            jnp.concatenate([v, next_block(v)], axis=1),
            jnp.concatenate([now_ref[blk, g], past_ref[blk, g]], axis=1), NT,
        )

    def lag_part(values, grad, blk, g):
        pairs = mm(values, jnp.concatenate([grad, next_block(grad)], axis=1), TN)
        joined = jnp.where(upper, pairs[:, :LANES], pairs[:, LANES:])
        total = joined[:8]
        for i in range(1, LANES // 8):
            total = total + pltpu.roll(joined[8 * i:8 * i + 8], LANES - 8 * i, 1)
        lag[pl.ds(pl.multiple_of((blk * groups + g) * 8, 8), 8)] = total

    def tap(q, gl, blk, k):
        one = wide[q, blk * tap_count + k, pl.ds(pl.multiple_of(gl * PER_GROUP, PER_GROUP), PER_GROUP)]
        return jnp.concatenate([one] * n, axis=0)

    def short_mix(x, q, gl, blk):
        total = tap(q, gl, blk, 0).astype(F32) * x.astype(F32)
        for k in range(1, tap_count):
            total = total + tap(q, gl, blk, k).astype(F32) * shift_past(x, k).astype(F32)
        return total.astype(BF16)

    def short_back(base, d, x, q, gl, blk):
        at = pl.ds(pl.multiple_of(gl * PER_GROUP, PER_GROUP), PER_GROUP)
        moved = [shift_next(d, k) for k in range(tap_count)]
        total = base.astype(F32)
        for k in range(tap_count):
            total = total + tap(q, gl, blk, k).astype(F32) * moved[k].astype(F32)
        sums = mm(fold, jnp.concatenate([m * x for m in moved], axis=1), NN)
        for k in range(tap_count):
            corr[blk * tap_count + k, at] = sums[:, k * LANES:(k + 1) * LANES]
        return total.astype(BF16)

    @pl.loop(0, chunks)
    def _(q):
        @pl.when(q <= hold)
        def _():
            arrive(q)

        for a in range(2):
            for b in range(n):
                turned = mm(eye, recv[a, q, b], NT).astype(BF16)
                xt[a, :, b * PER_GROUP:(b + 1) * PER_GROUP, :] = turned.reshape(
                    per_chunk, PER_GROUP, LANES
                )

        @pl.loop(0, per_chunk // batch)
        def _(step):
            local = [step * batch + u for u in range(batch)]
            every = range(batch)
            glob = [q * per_chunk + gl for gl in local]
            top = [xt[1, gl] for gl in local]
            src = [xt[0, gl] for gl in local]
            dmix_two = [anti(top[u], 1, glob[u]).astype(BF16) for u in every]
            mixed_one = [short_mix(src[u], q, local[u], 0) for u in every]
            long_one = [causal(mixed_one[u], 0, glob[u]) for u in every]
            middle = [(src[u].astype(F32) + long_one[u]).astype(BF16) for u in every]
            middle_grad = [
                short_back(top[u], dmix_two[u], middle[u], q, local[u], 1) for u in every
            ]
            dmix_one = [anti(middle_grad[u], 0, glob[u]).astype(BF16) for u in every]
            mixed_two = [short_mix(middle[u], q, local[u], 1) for u in every]
            for u in every:
                lag_part(mixed_two[u], top[u], 1, glob[u])
            for u in every:
                ot[local[u]] = short_back(middle_grad[u], dmix_one[u], src[u], q, local[u], 0)
            for u in every:
                lag_part(mixed_one[u], middle_grad[u], 0, glob[u])

        @pl.when(stage > 0)
        def _():
            for b in range(n):
                piece = ot[:, b * PER_GROUP:(b + 1) * PER_GROUP, :].reshape(square)
                obuf[q, b] = mm(eye, piece, NT).astype(BF16)
            for j in range(2):
                out_copy(q, j, flip(me, j), me).start()

        @pl.when(q == hold)
        def _():
            for later in range(hold + 1, chunks):
                arrive(later)

            @pl.when(stage > 0)
            def _():
                for earlier in range(hold + 1):
                    send_far(earlier)

        @pl.when((q > hold) & (stage > 0))
        def _():
            send_far(q)

        ones = jnp.ones((8, 2 * LANES), BF16)
        for blk in range(2):
            for k in range(tap_count):
                part = corr[blk * tap_count + k]
                high = part.astype(BF16)
                low = (part - high.astype(F32)).astype(BF16)
                summed = mm(ones, jnp.concatenate([high, low], axis=1), NT)
                short_ref[k, blk:blk + 1, pl.ds(pl.multiple_of(q * LANES, LANES), LANES)] = (
                    summed[:1] * factor
                )

    total = lag[pl.ds(0, 2 * groups, stride=8), :]
    for r in range(1, 8):
        total = total + pltpu.roll(lag[pl.ds(r, 2 * groups, stride=8), :], LANES - r, 1)
    total = total * factor
    long_ref[0] = total[:groups]
    long_ref[1] = total[groups:]

    @pl.loop(0, chunks)
    def _(q):
        for j in range(1, n):
            for a in range(2):
                in_copy(a, q, j, flip(me, j), me).wait_send()

    @pl.when(stage > 0)
    def _():
        @pl.loop(0, chunks)
        def _(q):
            for j in range(n):
                out_copy(q, j, flip(me, j), me).wait_send()

    @pl.when(stage < pipes - 1)
    def _():
        @pl.loop(0, chunks)
        def _(q):
            for j in range(n):
                out_copy(q, j, flip(me, j), flip(me, j)).wait_recv()


def finish(pipes, passed_ref, short_ref, long_ref, out_ref, short_out, long_out,
           rows_ref, short_buf, long_buf, in_sem, out_sem, small_sem):
    stage = lax.axis_index("pipe")
    parts = in_sem.shape[0]
    size = passed_ref.shape[0] // parts

    def piece(i):
        return pl.ds(i * size, size)

    def load(i):
        return pltpu.make_async_copy(passed_ref.at[piece(i)], rows_ref.at[piece(i)], in_sem.at[i])

    def store(i):
        return pltpu.make_async_copy(rows_ref.at[piece(i)], out_ref.at[piece(i)], out_sem.at[i])

    small_in = [
        pltpu.make_async_copy(short_ref, short_buf, small_sem.at[0]),
        pltpu.make_async_copy(long_ref, long_buf, small_sem.at[1]),
    ]
    small_out = [
        pltpu.make_async_copy(short_buf, short_out, small_sem.at[2]),
        pltpu.make_async_copy(long_buf, long_out, small_sem.at[3]),
    ]
    for copy in small_in:
        copy.start()

    @pl.when(stage < pipes - 1)
    def _():
        for i in range(parts):
            load(i).start()
        for i in range(parts):
            load(i).wait()
            store(i).start()

    @pl.when(stage == pipes - 1)
    def _():
        rows_ref[...] = jnp.zeros_like(rows_ref)
        for i in range(parts):
            store(i).start()

    for arrived, leaving in zip(small_in, small_out):
        arrived.wait()
        leaving.start()
    for copy in small_out:
        copy.wait()
    for i in range(parts):
        store(i).wait()


def body(n, pipes, section_input, out_grad, short_filter, long_filter):
    rows, channels = section_input.shape[1:]
    tap_count = short_filter.shape[2]
    groups, taps = long_filter.shape[2:]
    width = channels // n
    chunks = width // LANES
    assert rows == LANES and taps == LANES and width == groups * PER_GROUP
    per_chunk = LANES // PER_GROUP
    batch = max(1, min(8, 64 // n))
    factor = float(rows * n) ** (-0.5)
    vmem = pl.BlockSpec(memory_space=pltpu.VMEM)
    anywhere = pl.BlockSpec(memory_space=pltpu.HBM)
    dma = pltpu.SemaphoreType.DMA
    parts, short_grad, long_grad = pl.pallas_call(
        functools.partial(kernel, n, pipes, chunks, tap_count, batch, factor),
        out_shape=(
            jax.ShapeDtypeStruct((rows, channels), BF16),
            jax.ShapeDtypeStruct((tap_count, 2, width), F32),
            jax.ShapeDtypeStruct((2, groups, taps), F32),
        ),
        in_specs=[anywhere, anywhere, vmem, vmem],
        out_specs=(anywhere, vmem, vmem),
        scratch_shapes=[
            pltpu.VMEM((2, chunks, n, LANES, LANES), BF16),
            pltpu.VMEM((2, chunks, n, LANES, LANES), BF16),
            pltpu.VMEM((2, per_chunk, n * PER_GROUP, LANES), BF16),
            pltpu.VMEM((per_chunk, n * PER_GROUP, LANES), BF16),
            pltpu.VMEM((chunks, n, LANES, LANES), BF16),
            pltpu.VMEM((chunks, 2 * tap_count, LANES, LANES), BF16),
            pltpu.VMEM((2, groups, LANES, LANES), BF16),
            pltpu.VMEM((2, groups, LANES, LANES), BF16),
            pltpu.VMEM((2 * tap_count, LANES, LANES), F32),
            pltpu.VMEM((2 * groups * 8, LANES), F32),
            pltpu.VMEM((2, groups, LANES), F32),
            dma((2, chunks, n)),
            dma((2, chunks, n)),
            dma((2, chunks, n)),
            dma((2, chunks)),
            dma((chunks, n)),
            dma((chunks, n)),
        ],
        compiler_params=pltpu.CompilerParams(
            collective_id=0, has_side_effects=True, vmem_limit_bytes=63 * 1024 * 1024
        ),
    )(section_input[0], out_grad[0], short_filter[0].transpose(1, 0, 2), long_filter[0])
    passed, short_grad, long_grad = pl.pallas_call(
        functools.partial(finish, pipes),
        out_shape=(
            jax.ShapeDtypeStruct((rows, channels), BF16),
            jax.ShapeDtypeStruct(short_grad.shape, F32),
            jax.ShapeDtypeStruct(long_grad.shape, F32),
        ),
        in_specs=[anywhere] * 3,
        out_specs=(anywhere,) * 3,
        scratch_shapes=[
            pltpu.VMEM((rows, channels), BF16),
            pltpu.VMEM(short_grad.shape, F32),
            pltpu.VMEM(long_grad.shape, F32),
            dma((8,)),
            dma((8,)),
            dma((4,)),
        ],
        compiler_params=pltpu.CompilerParams(vmem_limit_bytes=63 * 1024 * 1024),
    )(parts, short_grad, long_grad)
    return passed[None], short_grad.transpose(1, 0, 2)[None], long_grad[None]


def solution(mesh):
    in_specs = (
        P("pipe", "dp", None),
        P("pipe", "dp", None),
        P("pipe", None, None, "dp"),
        P("pipe", None, "dp", None),
    )
    out_specs = (P("pipe", "dp", None), P("pipe", None, None, "dp"), P("pipe", None, "dp", None))
    run = functools.partial(body, mesh.shape["dp"], mesh.shape["pipe"])
    return jax.shard_map(run, mesh=mesh, in_specs=in_specs, out_specs=out_specs, check_vma=False)
```

```python
import functools

import jax
import jax.numpy as jnp
from jax import lax
from jax.experimental import pallas as pl
from jax.experimental.pallas import tpu as pltpu
from jax.sharding import PartitionSpec as P

MESH = pl.DeviceIdType.MESH
LANES = 128
PER_GROUP = 16
F32 = jnp.float32
BF16 = jnp.bfloat16
NT = (((1,), (1,)), ((), ()))
NN = (((1,), (0,)), ((), ()))
TN = (((0,), (0,)), ((), ()))


def mm(a, b, dims):
    return lax.dot_general(a, b, dims, preferred_element_type=F32)


def lanes_of(rows):
    return lax.broadcasted_iota(jnp.int32, (rows, LANES), 1)


def past_block(x):
    return jnp.concatenate([jnp.zeros((PER_GROUP, LANES), x.dtype), x[:-PER_GROUP]], axis=0)


def next_block(x):
    return jnp.concatenate([x[PER_GROUP:], jnp.zeros((PER_GROUP, LANES), x.dtype)], axis=0)


def shift_past(x, k):
    if k == 0:
        return x
    rolled = pltpu.roll(x, k, 1)
    return jnp.where(lanes_of(x.shape[0]) < k, past_block(rolled), rolled)


def shift_next(x, k):
    if k == 0:
        return x
    rolled = pltpu.roll(x, LANES - k, 1)
    return jnp.where(lanes_of(x.shape[0]) < LANES - k, rolled, next_block(rolled))


def flip(index, mask):
    out = index
    bit = 1
    while bit <= mask:
        if mask & bit:
            out = out + bit - 2 * bit * lax.rem(lax.div(index, bit), 2)
        bit *= 2
    return out


def orders(n):
    far = list(range(1, n // 2))
    later = far[1:] + far[:1]
    even = [2 * m for m in far] + [2 * m + 1 for m in far]
    odd = [2 * m for m in later] + [2 * m + 1 for m in later]
    return list(zip(even + [1], odd + [1]))


def kernel(n, pipes, chunks, tap_count, batch, factor,
           x_ref, g_ref, sf_ref, lf_ref,
           out_ref, short_ref, long_ref,
           recv, xt, ot, obuf, wide, now_ref, past_ref, corr, lag, lf_wide, mix_ref, back_ref,
           send_sem, recv_sem, local_sem, osend_sem, orecv_sem):
    stage = lax.axis_index("pipe")
    me = lax.axis_index("dp")
    rows = x_ref.shape[0]
    width = chunks * LANES
    per_chunk = LANES // PER_GROUP
    groups = chunks * per_chunk

    barrier = pltpu.get_barrier_semaphore()
    for j in range(1, n):
        pl.semaphore_signal(barrier, inc=1, device_id=(stage, lax.rem(me + j, n)), device_id_type=MESH)

    @pl.when(stage < pipes - 1)
    def _():
        for j in range(n):
            pl.semaphore_signal(barrier, inc=1, device_id=(stage + 1, j), device_id_type=MESH)

    pl.semaphore_wait(barrier, n - 1 + n * jnp.minimum(stage, 1))

    def columns(device, q):
        return pl.ds(pl.multiple_of(device * width + q * LANES, LANES), LANES)

    core = lax.rem(me, 2)

    def pick(step):
        first, second = step
        return (
            first + core * (second - first),
            flip(me, first) + core * (flip(me, second) - flip(me, first)),
        )

    def in_copy(a, q, j, to, slot):
        return pltpu.make_async_remote_copy(
            src_ref=(x_ref, g_ref)[a].at[:, columns(to, q)],
            dst_ref=recv.at[a, q, slot],
            send_sem=send_sem.at[a, q, j],
            recv_sem=recv_sem.at[a, q, j],
            device_id=(stage, to),
            device_id_type=MESH,
        )

    def own_copy(a, q):
        return pltpu.make_async_copy(
            (x_ref, g_ref)[a].at[:, columns(me, q)], recv.at[a, q, me], local_sem.at[a, q]
        )

    def out_copy(q, j, to, source):
        return pltpu.make_async_remote_copy(
            src_ref=obuf.at[q, to],
            dst_ref=out_ref.at[:, columns(source, q)],
            send_sem=osend_sem.at[q, j],
            recv_sem=orecv_sem.at[q, j],
            device_id=(stage - 1, to),
            device_id_type=MESH,
        )

    @pl.loop(0, chunks)
    def _(q):
        for step in orders(n):
            for a in range(2):
                in_copy(a, q, *pick(step), me).start()
        for a in range(2):
            own_copy(a, q).start()

    square = (LANES, LANES)
    row_pos = lax.broadcasted_iota(jnp.int32, square, 0)
    col_pos = lax.broadcasted_iota(jnp.int32, square, 1)
    eye = (row_pos == col_pos).astype(BF16)
    upper = row_pos <= col_pos

    @pl.loop(0, chunks)
    def _(q):
        for blk in range(2):
            taps_q = sf_ref[:, blk, pl.ds(pl.multiple_of(q * LANES, LANES), LANES)]
            for k in range(tap_count):
                spread = jnp.broadcast_to(taps_q[k:k + 1].astype(F32), square).astype(BF16)
                wide[q, blk * tap_count + k] = mm(eye, spread, NT).astype(BF16)

    wide_row = lax.broadcasted_iota(jnp.int32, (LANES, 2 * LANES), 0)
    wide_col = lax.broadcasted_iota(jnp.int32, (LANES, 2 * LANES), 1)
    for k in range(tap_count):
        at = pl.ds(k * LANES, LANES)
        mix_ref[at] = (wide_col == wide_row + k).astype(BF16)
        away = jnp.where(wide_col < LANES, wide_col + k, wide_col - 2 * LANES + k)
        back_ref[at] = (wide_row == away).astype(BF16)
    fold_row = lax.broadcasted_iota(jnp.int32, (PER_GROUP, n * PER_GROUP), 0)
    fold_col = lax.broadcasted_iota(jnp.int32, (PER_GROUP, n * PER_GROUP), 1)
    fold = (lax.rem(fold_col, PER_GROUP) == fold_row).astype(BF16)

    lf_wide[...] = lf_ref[...].astype(F32)

    @pl.loop(0, groups)
    def _(g):
        for blk in range(2):
            filt = lf_wide[blk, pl.ds(g, 1)]
            circ = pltpu.roll(jnp.broadcast_to(filt, square), 0, 1, stride=1, stride_axis=0)
            now_ref[blk, g] = jnp.where(upper, circ, 0.0).astype(BF16)
            past_ref[blk, g] = jnp.where(upper, 0.0, circ).astype(BF16)

    def causal(v, blk, g):
        return mm(
            jnp.concatenate([v, past_block(v)], axis=1),
            jnp.concatenate([now_ref[blk, g], past_ref[blk, g]], axis=0), NN,
        )

    def anti(v, blk, g):
        return mm(
            jnp.concatenate([v, next_block(v)], axis=1),
            jnp.concatenate([now_ref[blk, g], past_ref[blk, g]], axis=1), NT,
        )

    def lag_part(values, grad, blk, g):
        pairs = mm(values, jnp.concatenate([grad, next_block(grad)], axis=1), TN)
        joined = jnp.where(upper, pairs[:, :LANES], pairs[:, LANES:])
        total = joined[:8]
        for i in range(1, LANES // 8):
            total = total + pltpu.roll(joined[8 * i:8 * i + 8], LANES - 8 * i, 1)
        lag[pl.ds(pl.multiple_of((blk * groups + g) * 8, 8), 8)] = total

    def tap(q, gl, blk, k):
        one = wide[q, blk * tap_count + k, pl.ds(pl.multiple_of(gl * PER_GROUP, PER_GROUP), PER_GROUP)]
        return jnp.concatenate([one] * n, axis=0)

    def weighted(x, q, gl, blk):
        return jnp.concatenate([tap(q, gl, blk, k) * x for k in range(tap_count)], axis=1)

    def short_mix(xs, q, local, blk):
        terms = jnp.concatenate([weighted(x, q, gl, blk) for x, gl in zip(xs, local)], axis=0)
        both = mm(terms, mix_ref[...], NN)
        size = n * PER_GROUP
        return [
            (both[u * size:(u + 1) * size, :LANES]
             + past_block(both[u * size:(u + 1) * size, LANES:])).astype(BF16)
            for u in range(len(xs))
        ]

    def short_back(bases, ds, q, local, blk):
        terms = jnp.concatenate([weighted(d, q, gl, blk) for d, gl in zip(ds, local)], axis=0)
        both = mm(terms, back_ref[...], NN)
        size = n * PER_GROUP
        return [
            (base.astype(F32) + both[u * size:(u + 1) * size, :LANES]
             + next_block(both[u * size:(u + 1) * size, LANES:])).astype(BF16)
            for u, base in enumerate(bases)
        ]

    def short_corr(d, x, gl, blk):
        at = pl.ds(pl.multiple_of(gl * PER_GROUP, PER_GROUP), PER_GROUP)
        prods = jnp.concatenate([shift_next(d, k) * x for k in range(tap_count)], axis=1)
        sums = mm(fold, prods, NN)
        for k in range(tap_count):
            corr[blk * tap_count + k, at] = sums[:, k * LANES:(k + 1) * LANES]

    @pl.loop(0, chunks)
    def _(q):
        for j in range(1, n):
            for a in range(2):
                in_copy(a, q, j, flip(me, j), flip(me, j)).wait_recv()
        for a in range(2):
            own_copy(a, q).wait()
        for a in range(2):
            for b in range(n):
                turned = mm(eye, recv[a, q, b], NT).astype(BF16)
                xt[a, :, b * PER_GROUP:(b + 1) * PER_GROUP, :] = turned.reshape(
                    per_chunk, PER_GROUP, LANES
                )

        @pl.loop(0, per_chunk // batch)
        def _(step):
            local = [step * batch + u for u in range(batch)]
            every = range(batch)
            glob = [q * per_chunk + gl for gl in local]
            top = [xt[1, gl] for gl in local]
            src = [xt[0, gl] for gl in local]
            dmix_two = [anti(top[u], 1, glob[u]).astype(BF16) for u in every]
            mixed_one = short_mix(src, q, local, 0)
            long_one = [causal(mixed_one[u], 0, glob[u]) for u in every]
            middle = [(src[u].astype(F32) + long_one[u]).astype(BF16) for u in every]
            middle_grad = short_back(top, dmix_two, q, local, 1)
            dmix_one = [anti(middle_grad[u], 0, glob[u]).astype(BF16) for u in every]
            mixed_two = short_mix(middle, q, local, 1)
            for u in every:
                short_corr(dmix_two[u], middle[u], local[u], 1)
            for u in every:
                lag_part(mixed_two[u], top[u], 1, glob[u])
            result = short_back(middle_grad, dmix_one, q, local, 0)
            for u in every:
                ot[local[u]] = result[u]
            for u in every:
                short_corr(dmix_one[u], src[u], local[u], 0)
            for u in every:
                lag_part(mixed_one[u], middle_grad[u], 0, glob[u])

        @pl.when(stage > 0)
        def _():
            for b in range(n):
                piece = ot[:, b * PER_GROUP:(b + 1) * PER_GROUP, :].reshape(square)
                obuf[q, b] = mm(eye, piece, NT).astype(BF16)
            for step in orders(n) + [(0, 0)]:
                out_copy(q, *pick(step), me).start()

        ones = jnp.ones((8, 2 * LANES), BF16)
        for blk in range(2):
            for k in range(tap_count):
                part = corr[blk * tap_count + k]
                high = part.astype(BF16)
                low = (part - high.astype(F32)).astype(BF16)
                summed = mm(ones, jnp.concatenate([high, low], axis=1), NT)
                short_ref[k, blk:blk + 1, pl.ds(pl.multiple_of(q * LANES, LANES), LANES)] = (
                    summed[:1] * factor
                )

    total = lag[pl.ds(0, 2 * groups, stride=8), :]
    for r in range(1, 8):
        total = total + pltpu.roll(lag[pl.ds(r, 2 * groups, stride=8), :], LANES - r, 1)
    total = total * factor
    long_ref[0] = total[:groups]
    long_ref[1] = total[groups:]

    @pl.loop(0, chunks)
    def _(q):
        for j in range(1, n):
            for a in range(2):
                in_copy(a, q, j, flip(me, j), me).wait_send()

    @pl.when(stage > 0)
    def _():
        @pl.loop(0, chunks)
        def _(q):
            for j in range(n):
                out_copy(q, j, flip(me, j), me).wait_send()

    @pl.when(stage < pipes - 1)
    def _():
        @pl.loop(0, chunks)
        def _(q):
            for j in range(n):
                out_copy(q, j, flip(me, j), flip(me, j)).wait_recv()


def finish(pipes, passed_ref, short_ref, long_ref, out_ref, short_out, long_out,
           rows_ref, short_buf, long_buf, in_sem, out_sem, small_sem):
    stage = lax.axis_index("pipe")
    parts = in_sem.shape[0]
    size = passed_ref.shape[0] // parts

    def piece(i):
        return pl.ds(i * size, size)

    def load(i):
        return pltpu.make_async_copy(passed_ref.at[piece(i)], rows_ref.at[piece(i)], in_sem.at[i])

    def store(i):
        return pltpu.make_async_copy(rows_ref.at[piece(i)], out_ref.at[piece(i)], out_sem.at[i])

    small_in = [
        pltpu.make_async_copy(short_ref, short_buf, small_sem.at[0]),
        pltpu.make_async_copy(long_ref, long_buf, small_sem.at[1]),
    ]
    small_out = [
        pltpu.make_async_copy(short_buf, short_out, small_sem.at[2]),
        pltpu.make_async_copy(long_buf, long_out, small_sem.at[3]),
    ]
    for copy in small_in:
        copy.start()

    @pl.when(stage < pipes - 1)
    def _():
        for i in range(parts):
            load(i).start()
        for i in range(parts):
            load(i).wait()
            store(i).start()

    @pl.when(stage == pipes - 1)
    def _():
        rows_ref[...] = jnp.zeros_like(rows_ref)
        for i in range(parts):
            store(i).start()

    for arrived, leaving in zip(small_in, small_out):
        arrived.wait()
        leaving.start()
    for copy in small_out:
        copy.wait()
    for i in range(parts):
        store(i).wait()


def body(n, pipes, section_input, out_grad, short_filter, long_filter):
    rows, channels = section_input.shape[1:]
    tap_count = short_filter.shape[2]
    groups, taps = long_filter.shape[2:]
    width = channels // n
    chunks = width // LANES
    assert rows == LANES and taps == LANES and width == groups * PER_GROUP
    per_chunk = LANES // PER_GROUP
    batch = max(1, min(4, 32 // n))
    factor = float(rows * n) ** (-0.5)
    vmem = pl.BlockSpec(memory_space=pltpu.VMEM)
    anywhere = pl.BlockSpec(memory_space=pltpu.HBM)
    dma = pltpu.SemaphoreType.DMA
    passed, short_grad, long_grad = pl.pallas_call(
        functools.partial(kernel, n, pipes, chunks, tap_count, batch, factor),
        out_shape=(
            jax.ShapeDtypeStruct((rows, channels), BF16),
            jax.ShapeDtypeStruct((tap_count, 2, width), F32),
            jax.ShapeDtypeStruct((2, groups, taps), F32),
        ),
        in_specs=[anywhere, anywhere, vmem, vmem],
        out_specs=(anywhere, vmem, vmem),
        scratch_shapes=[
            pltpu.VMEM((2, chunks, n, LANES, LANES), BF16),
            pltpu.VMEM((2, per_chunk, n * PER_GROUP, LANES), BF16),
            pltpu.VMEM((per_chunk, n * PER_GROUP, LANES), BF16),
            pltpu.VMEM((chunks, n, LANES, LANES), BF16),
            pltpu.VMEM((chunks, 2 * tap_count, LANES, LANES), BF16),
            pltpu.VMEM((2, groups, LANES, LANES), BF16),
            pltpu.VMEM((2, groups, LANES, LANES), BF16),
            pltpu.VMEM((2 * tap_count, LANES, LANES), F32),
            pltpu.VMEM((2 * groups * 8, LANES), F32),
            pltpu.VMEM((2, groups, LANES), F32),
            pltpu.VMEM((tap_count * LANES, 2 * LANES), BF16),
            pltpu.VMEM((tap_count * LANES, 2 * LANES), BF16),
            dma((2, chunks, n)),
            dma((2, chunks, n)),
            dma((2, chunks)),
            dma((chunks, n)),
            dma((chunks, n)),
        ],
        compiler_params=pltpu.CompilerParams(
            collective_id=0, has_side_effects=True, vmem_limit_bytes=63 * 1024 * 1024
        ),
    )(section_input[0], out_grad[0], short_filter[0].transpose(1, 0, 2), long_filter[0])
    passed, short_grad, long_grad = pl.pallas_call(
        functools.partial(finish, pipes),
        out_shape=(
            jax.ShapeDtypeStruct((rows, channels), BF16),
            jax.ShapeDtypeStruct(short_grad.shape, F32),
            jax.ShapeDtypeStruct(long_grad.shape, F32),
        ),
        in_specs=[anywhere] * 3,
        out_specs=(anywhere,) * 3,
        scratch_shapes=[
            pltpu.VMEM((rows, channels), BF16),
            pltpu.VMEM(short_grad.shape, F32),
            pltpu.VMEM(long_grad.shape, F32),
            dma((8,)),
            dma((8,)),
            dma((4,)),
        ],
        compiler_params=pltpu.CompilerParams(vmem_limit_bytes=63 * 1024 * 1024),
    )(passed, short_grad, long_grad)
    return passed[None], short_grad.transpose(1, 0, 2)[None], long_grad[None]


def solution(mesh):
    in_specs = (
        P("pipe", "dp", None),
        P("pipe", "dp", None),
        P("pipe", None, None, "dp"),
        P("pipe", None, "dp", None),
    )
    out_specs = (P("pipe", "dp", None), P("pipe", None, None, "dp"), P("pipe", None, "dp", None))
    run = functools.partial(body, mesh.shape["dp"], mesh.shape["pipe"])
    return jax.shard_map(run, mesh=mesh, in_specs=in_specs, out_specs=out_specs, check_vma=False)
```
